32 devices in a mesh: seq: 2 (over x), fsdp: 16 (over z, y, core).
Axes of the slice: x: 2, y: 2, z: 4, core: 2. Of those that a mesh axis runs over, the one named last changes fastest.
Arguments:
- tokens: bfloat16 [16, 1024, 1536], P('fsdp', 'seq'), may hold values from -6 to 6
- cotangent: bfloat16 [16, 1024, 1536], P('fsdp', 'seq'), may hold values from -6 to 6
- segment_ids: int32 [16, 1024], P('fsdp', 'seq'), may hold values from 0 to 8, as said below
- route_ids: int32 [16, 1024, 4], P('fsdp', 'seq'), may hold values from 0 to 7, all different within a row; in each aligned block of 512 rows (0 to 511, 512 to 1023, ..., all dimensions but the last counted through in order) at most 320 rows name the same one
- query_key_value_weight: float32 [1536, 2048], P(('seq', 'fsdp')), may hold values from -0.15625 to 0.15625
- out_weight: float32 [1536, 1536], P(('seq', 'fsdp')), may hold values from -1.25 to 1.25
- router_weight: float32 [1536, 8], P(('seq', 'fsdp')), may hold values from -0.078125 to 0.078125
- expert_in: float32 [8, 1536, 1536], P(None, ('seq', 'fsdp')), may hold values from -0.15625 to 0.15625
- expert_down: float32 [8, 768, 1536], P(None, ('seq', 'fsdp')), may hold values from -1.75 to 1.75
- norm_gains: float32 [1536, 2], P(('seq', 'fsdp')), may hold values from 0.3 to 2.5, as said below
- query_key_value_moment: float32 [1536, 2048], P(('seq', 'fsdp')), may hold values from -0.00024414062 to 0.00024414062
- out_moment: float32 [1536, 1536], P(('seq', 'fsdp')), may hold values from -6.1035156e-05 to 6.1035156e-05
- router_moment: float32 [1536, 8], P(('seq', 'fsdp')), may hold values from -0.00024414062 to 0.00024414062
- in_moment: float32 [8, 1536, 1536], P(None, ('seq', 'fsdp')), may hold values from -0.00024414062 to 0.00024414062
- down_moment: float32 [8, 768, 1536], P(None, ('seq', 'fsdp')), may hold values from -9.536743e-06 to 9.536743e-06
- gains_moment: float32 [1536, 2], P(('seq', 'fsdp')), may hold values from -0.0008544922 to 0.0008544922
- query_key_value_second: float32 [1536, 2048], P(('seq', 'fsdp')), may hold values from 1.5665672e-09 to 6.207153e-09
- out_second: float32 [1536, 1536], P(('seq', 'fsdp')), may hold values from 7.0938894e-11 to 2.8079977e-10
- router_second: float32 [1536, 8], P(('seq', 'fsdp')), may hold values from 1.5665672e-09 to 6.207153e-09
- in_second: float32 [8, 1536, 1536], P(None, ('seq', 'fsdp')), may hold values from 1.5665672e-09 to 6.207153e-09
- down_second: float32 [8, 768, 1536], P(None, ('seq', 'fsdp')), may hold values from 1.8917038e-12 to 7.3894675e-12
- gains_second: float32 [1536, 2], P(('seq', 'fsdp')), may hold values from 1.3892199e-08 to 5.6159955e-08
Outputs:
- output: bfloat16 [16, 1024, 1536], P('fsdp', 'seq')
- input_grad: bfloat16 [16, 1024, 1536], P('fsdp', 'seq')
- grad_norm: float32 [], replicated
- qkv_new: float32 [1536, 2048], P(('seq', 'fsdp'))
- out_new: float32 [1536, 1536], P(('seq', 'fsdp'))
- router_new: float32 [1536, 8], P(('seq', 'fsdp'))
- in_new: float32 [8, 1536, 1536], P(None, ('seq', 'fsdp'))
- down_new: float32 [8, 768, 1536], P(None, ('seq', 'fsdp'))
- gains_new: float32 [1536, 2], P(('seq', 'fsdp'))
- qkv_moment_new: float32 [1536, 2048], P(('seq', 'fsdp'))
- out_moment_new: float32 [1536, 1536], P(('seq', 'fsdp'))
- router_moment_new: float32 [1536, 8], P(('seq', 'fsdp'))
- in_moment_new: float32 [8, 1536, 1536], P(None, ('seq', 'fsdp'))
- down_moment_new: float32 [8, 768, 1536], P(None, ('seq', 'fsdp'))
- gains_moment_new: float32 [1536, 2], P(('seq', 'fsdp'))
- qkv_second_new: float32 [1536, 2048], P(('seq', 'fsdp'))
- out_second_new: float32 [1536, 1536], P(('seq', 'fsdp'))
- router_second_new: float32 [1536, 8], P(('seq', 'fsdp'))
- in_second_new: float32 [8, 1536, 1536], P(None, ('seq', 'fsdp'))
- down_second_new: float32 [8, 768, 1536], P(None, ('seq', 'fsdp'))
- gains_second_new: float32 [1536, 2], P(('seq', 'fsdp'))
The draws below stay inside these ranges and needn't reach their ends.
Inputs may be any that keep to these rules, and one draw needn't show every extreme that they name: `segment_ids`: segment numbers start at 0 in every pack and never fall along it. `route_ids`: each row names 4 different experts. The rows of one device (aligned blocks of 512 rows in pack order) name no expert more than 320 times, a bound that some block reaches. `norm_gains`: positive gains.
All inputs are finite; a program needn't handle non-finite values.
Results may differ from the reference program's by a relative error of at most 0.019.
The reference program's roundings to bfloat16 on the way count: a program that leaves them out, or rounds other values in their place, can miss the bound.
Values may be sent and summed in bfloat16 or wider, within the bound.
No kernel may reach another device: no remote copies, remote signals or barrier semaphores. Data moves between devices by JAX's collectives and lax.ppermute only.
A program may use at most 448 MiB of HBM per device.

```python
import math
import jax
import jax.numpy as jnp
import numpy as np
from jax import lax

MODEL_DIMENSION = 1536
QUERY_HEADS = 12
KEY_VALUE_HEADS = 2
HEAD_DIMENSION = 128
F = 768
EXPERTS = 8
TOPK = 4
STEP = 10
TOK_DEV = 512
LEN = 1024
PACKS = 16
CAP = 320
LAYER_PARAMETERS = 33831936


def draw_segment_ids(key, part):
    key = jax.random.fold_in(key, 11)
    low_edge = LEN * 3 // 8
    high_edge = LEN * 5 // 8
    spaces = low_edge - 1 + (LEN - 1 - high_edge)
    picks = jax.random.randint(key, (PACKS, 8), 0, spaces)
    cuts = 1 + picks + jnp.where(1 + picks >= low_edge, high_edge - low_edge + 1, 0)
    places = jnp.arange(LEN, dtype=jnp.int32)
    return jnp.sum((cuts[:, None, :] <= places[None, :, None]).astype(jnp.int32), axis=2).astype(jnp.int32)


def draw_norm_gains(key, part):
    key = jax.random.fold_in(key, 23)
    ramp = jnp.arange(MODEL_DIMENSION, dtype=jnp.float32) / (MODEL_DIMENSION - 1)
    base = 0.6 + 1.2 * ramp
    noise = jax.random.uniform(key, (MODEL_DIMENSION, 2), jnp.float32, 0.85, 1.15)
    return (base[:, None] * noise).astype(jnp.float32)


def block_levels(rng, shape, shards, least, largest):
    def one(axis_at, shards_of):
        draws = jax.random.uniform(jax.random.fold_in(jax.random.fold_in(rng, 6), axis_at), (shards_of,), jnp.float32, least / len(shards), largest / len(shards))
        return jnp.repeat(jnp.exp(draws), shape[axis_at] // shards_of).reshape((-1,) + (1,) * (len(shape) - axis_at - 1))

    level = one(*shards[0])
    for cut in shards[1:]:
        level = level * one(*cut)
    return level


def deal_out(own_key, own, number, rows, count, top, limit, lean):
    sequence = jax.random.permutation(own_key, count)
    heavy_load, common = portions_of(count, rows * top, limit, lean, True), portions_of(count, rows * top, limit, lean, False)
    places = jnp.arange(count)

    def named(lengths, offset_by):
        used = int((lengths > 0).sum())
        fixed = max(1, used // 4)
        moved = fixed + (places - fixed + offset_by * (used - fixed)) % max(1, count - fixed)
        return jnp.zeros((count,), jnp.int32).at[sequence[jnp.where(places < fixed, places, moved)]].set(jnp.asarray(lengths, jnp.int32))

    lengths = jnp.where(number % 4 == 0, named(heavy_load, number // 4), named(common, number - number // 4 - 1))
    mixed = jax.random.permutation(jax.random.fold_in(own, 3), count)
    donor, receiver = mixed[0:count // 2 * 2:2], mixed[1:count // 2 * 2:2]
    slack = jnp.minimum(lengths[donor] - 1, limit - lengths[receiver]) // 2
    slack = jnp.where((donor == sequence[0]) | (receiver == sequence[0]) | (lengths[receiver] == 0), 0, jnp.maximum(slack, 0))
    moved = jax.random.randint(jax.random.fold_in(own, 4), (count // 2,), 0, 1 << 20) % (slack + 1)
    lengths = lengths.at[donor].add(-moved).at[receiver].add(moved)
    members = jnp.searchsorted(jnp.cumsum(lengths), jnp.arange(rows * top), side="right").astype(jnp.int32)
    grid = members.reshape(top, rows).T
    grid = grid[jax.random.permutation(jax.random.fold_in(own, 1), rows)]
    offset_by = jax.random.randint(jax.random.fold_in(own, 2), (rows, 1), 0, top)
    return jnp.take_along_axis(grid, (jnp.arange(top)[None, :] + offset_by) % top, axis=1)


def portions_of(number_of, total, bound, lean, full):
    loads = [(1 << 20) // math.isqrt(grade ** lean) + 1 for grade in range(1, number_of + 1)]
    largest = bound if full else min(bound, max(-(-total // number_of), total * loads[0] // sum(loads)))
    least = 1 if total - largest >= number_of - 1 else 0
    given, surplus = [largest] + [least] * (number_of - 1), total - largest - least * (number_of - 1)
    while surplus > 0:
        candidates = [i for i in range(1, number_of) if given[i] < largest] or [i for i in range(1, number_of) if given[i] < bound]
        mass, left = sum([loads[i] for i in candidates]), surplus
        for i in candidates:
            more = min(bound - given[i], max(1, left * loads[i] // mass), surplus)
            given[i] = given[i] + more
            surplus = surplus - more
    return np.array(given)


def centred(key, shape, scale, limit, pieces=(), held_as=jnp.bfloat16):
    level = block_levels(key, shape, pieces, -0.22, 0.18) if pieces else 1.0
    drawn = jax.random.normal(key, shape, jnp.float32) * scale * level
    return jnp.minimum(jnp.maximum(drawn, -limit), limit).astype(held_as)


def setup_inputs(seed: int = 0) -> dict:
    seeds = jax.random.split(jax.random.key(seed), 23)
    tokens = centred(seeds[0], (PACKS, LEN, MODEL_DIMENSION), 1.0, 6.0, ((0, 16), (1, 2)))
    cotangent = centred(seeds[1], (PACKS, LEN, MODEL_DIMENSION), 1.0, 6.0, ((0, 16), (1, 2)))
    segment_ids = draw_segment_ids(jax.random.fold_in(seeds[22], 71), 0)
    route_ids_keys = jax.random.split(jax.random.fold_in(seeds[3], 1), PACKS * LEN // TOK_DEV)
    route_ids_turns = jax.random.permutation(jax.random.fold_in(seeds[3], 3), PACKS * LEN // TOK_DEV)
    route_ids = jax.vmap(lambda own, number: deal_out(jax.random.fold_in(seeds[3], 2), own, number, TOK_DEV, EXPERTS, TOPK, CAP, 1))(route_ids_keys, route_ids_turns).reshape((PACKS, LEN, TOPK))
    query_key_value_weight = centred(seeds[4], (MODEL_DIMENSION, (QUERY_HEADS + 2 * KEY_VALUE_HEADS) * HEAD_DIMENSION), MODEL_DIMENSION ** -0.5, 0.15625, ((0, 32),), jnp.float32)
    out_weight = centred(seeds[5], (QUERY_HEADS * HEAD_DIMENSION, MODEL_DIMENSION), (QUERY_HEADS * HEAD_DIMENSION // 64) ** -0.5, 1.25, ((0, 32),), jnp.float32)
    router_weight = centred(seeds[6], (MODEL_DIMENSION, EXPERTS), (4 * MODEL_DIMENSION) ** -0.5, 0.078125, ((0, 32),), jnp.float32)
    expert_in = centred(seeds[7], (EXPERTS, MODEL_DIMENSION, 2 * F), MODEL_DIMENSION ** -0.5, 0.15625, ((1, 32),), jnp.float32)
    expert_down = centred(seeds[8], (EXPERTS, F, MODEL_DIMENSION), (F // 64) ** -0.5, 1.75, ((1, 32),), jnp.float32)
    norm_gains = draw_norm_gains(jax.random.fold_in(seeds[22], 71), 0)
    query_key_value_moment = centred(seeds[10], (MODEL_DIMENSION, (QUERY_HEADS + 2 * KEY_VALUE_HEADS) * HEAD_DIMENSION), (0.11 / LAYER_PARAMETERS ** 0.5), 0.00024414062, ((0, 32),), jnp.float32)
    out_moment = centred(seeds[11], (QUERY_HEADS * HEAD_DIMENSION, MODEL_DIMENSION), (0.023 / LAYER_PARAMETERS ** 0.5), 6.103515625e-05, ((0, 32),), jnp.float32)
    router_moment = centred(seeds[12], (MODEL_DIMENSION, EXPERTS), (0.11 / LAYER_PARAMETERS ** 0.5), 0.00024414062, ((0, 32),), jnp.float32)
    in_moment = centred(seeds[13], (EXPERTS, MODEL_DIMENSION, 2 * F), (0.11 / LAYER_PARAMETERS ** 0.5), 0.00024414062, ((1, 32),), jnp.float32)
    down_moment = centred(seeds[14], (EXPERTS, F, MODEL_DIMENSION), (0.0038 / LAYER_PARAMETERS ** 0.5), 9.5367431640625e-06, ((1, 32),), jnp.float32)
    gains_moment = centred(seeds[15], (MODEL_DIMENSION, 2), (0.33 / LAYER_PARAMETERS ** 0.5), 0.0008544922, ((0, 32),), jnp.float32)
    query_key_value_second = jnp.clip(jnp.exp(math.log(6.207153013804145e-09) - 1.3768156 * jax.random.uniform(seeds[16], (MODEL_DIMENSION, (QUERY_HEADS + 2 * KEY_VALUE_HEADS) * HEAD_DIMENSION), jnp.float32) ** block_levels(seeds[16], (MODEL_DIMENSION, (QUERY_HEADS + 2 * KEY_VALUE_HEADS) * HEAD_DIMENSION), ((0, 32),), -0.2, 0.2)), 1.566567209287939e-09, 6.207153013804145e-09)
    out_second = jnp.clip(jnp.exp(math.log(2.807997723230926e-10) - 1.375823 * jax.random.uniform(seeds[17], (QUERY_HEADS * HEAD_DIMENSION, MODEL_DIMENSION), jnp.float32) ** block_levels(seeds[17], (QUERY_HEADS * HEAD_DIMENSION, MODEL_DIMENSION), ((0, 32),), -0.2, 0.2)), 7.093889364817585e-11, 2.807997723230926e-10)
    router_second = jnp.clip(jnp.exp(math.log(6.207153013804145e-09) - 1.3768156 * jax.random.uniform(seeds[18], (MODEL_DIMENSION, EXPERTS), jnp.float32) ** block_levels(seeds[18], (MODEL_DIMENSION, EXPERTS), ((0, 32),), -0.2, 0.2)), 1.566567209287939e-09, 6.207153013804145e-09)
    in_second = jnp.clip(jnp.exp(math.log(6.207153013804145e-09) - 1.3768156 * jax.random.uniform(seeds[19], (EXPERTS, MODEL_DIMENSION, 2 * F), jnp.float32) ** block_levels(seeds[19], (EXPERTS, MODEL_DIMENSION, 2 * F), ((1, 32),), -0.2, 0.2)), 1.566567209287939e-09, 6.207153013804145e-09)
    down_second = jnp.clip(jnp.exp(math.log(7.389467510110492e-12) - 1.3625778 * jax.random.uniform(seeds[20], (EXPERTS, F, MODEL_DIMENSION), jnp.float32) ** block_levels(seeds[20], (EXPERTS, F, MODEL_DIMENSION), ((1, 32),), -0.2, 0.2)), 1.8917038074883763e-12, 7.389467510110492e-12)
    gains_second = jnp.clip(jnp.exp(math.log(5.615995490870773e-08) - 1.3968765 * jax.random.uniform(seeds[21], (MODEL_DIMENSION, 2), jnp.float32) ** block_levels(seeds[21], (MODEL_DIMENSION, 2), ((0, 32),), -0.2, 0.2)), 1.3892199390852511e-08, 5.615995490870773e-08)
    return dict(tokens=tokens, cotangent=cotangent, segment_ids=segment_ids, route_ids=route_ids, query_key_value_weight=query_key_value_weight, out_weight=out_weight, router_weight=router_weight, expert_in=expert_in, expert_down=expert_down, norm_gains=norm_gains, query_key_value_moment=query_key_value_moment, out_moment=out_moment, router_moment=router_moment, in_moment=in_moment, down_moment=down_moment, gains_moment=gains_moment, query_key_value_second=query_key_value_second, out_second=out_second, router_second=router_second, in_second=in_second, down_second=down_second, gains_second=gains_second)


@jax.custom_vjp
def low(v):
    return lax.optimization_barrier(v.astype(jnp.bfloat16)).astype(jnp.float32)

@jax.custom_vjp
def low_back(v):
    return v

def low_keep(v):
    return (low(v), None)

def low_pass(kept, grad):
    return (grad,)

def back_keep(v):
    return (v, None)

def back_low(kept, grad):
    return (low(grad),)
low.defvjp(low_keep, low_pass)
low_back.defvjp(back_keep, back_low)
PRECISE = lax.Precision.HIGHEST
NORM_EPS = 1e-06
CLIP_NORM = 1.0
BETA_ONE = 0.9
BETA_TWO = 0.95
ADAM_EPS = 1e-08
DECAY_RATE = 0.1
ROPE_BASE = 10000.0
MASKED_SCORE = -1e+30

def rms_scale(values):
    return lax.rsqrt(lax.optimization_barrier(jnp.mean(values * values, axis=-1, keepdims=True)) + NORM_EPS)

def rotation_embedding(values, token_positions):
    half_size = values.shape[-1] // 2
    frequency = ROPE_BASE ** (-2.0 * jnp.arange(half_size, dtype=jnp.float32) / values.shape[-1])
    angles = token_positions[:, None] * frequency[None, :]
    cosine = jnp.cos(angles)[:, None, :]
    sine_part = jnp.sin(angles)[:, None, :]
    former = values[..., :half_size]
    latter = values[..., half_size:]
    return jnp.concatenate([former * cosine - latter * sine_part, latter * cosine + former * sine_part], axis=-1)

def slot_tables(route_rows):
    flat_routes = route_rows.reshape(-1).astype(jnp.int32)
    assigned = flat_routes.shape[0]
    chosen = (flat_routes[:, None] == jnp.arange(EXPERTS, dtype=jnp.int32)[None, :]).astype(jnp.int32)
    running = jnp.cumsum(chosen, axis=0)
    slot_index = lax.optimization_barrier(jnp.sum(running * chosen, axis=1)) - 1
    targets = (flat_routes * CAP + slot_index).astype(jnp.int32)
    slot_owner = jnp.full((EXPERTS * CAP,), assigned, jnp.int32).at[targets].set(jnp.arange(assigned, dtype=jnp.int32))
    return (targets, slot_owner)

def step_sizes():
    return (MODEL_DIMENSION ** (-0.5), (QUERY_HEADS * HEAD_DIMENSION // 64) ** (-0.5), (4 * MODEL_DIMENSION) ** (-0.5), MODEL_DIMENSION ** (-0.5), (F // 64) ** (-0.5), 0.3)

def adam_step(weight, gradient, moment, second, step_size, decay_value):
    moment_new = BETA_ONE * moment + (1.0 - BETA_ONE) * gradient
    second_new = BETA_TWO * second + (1.0 - BETA_TWO) * gradient * gradient
    corrected = moment_new / (1.0 - BETA_ONE ** STEP) / (jnp.sqrt(second_new / (1.0 - BETA_TWO ** STEP)) + ADAM_EPS)
    return (weight - step_size * (corrected + decay_value * weight), moment_new, second_new)

def update_all(weights, gradients, moments, seconds, factor):
    sizes_list = step_sizes()
    decays = (DECAY_RATE, DECAY_RATE, DECAY_RATE, DECAY_RATE, DECAY_RATE, 0.0)
    new_weights = []
    new_moments = []
    new_seconds = []
    for position in range(6):
        weight_new, moment_new, second_new = adam_step(weights[position], gradients[position] * factor, moments[position], seconds[position], sizes_list[position], decays[position])
        new_weights.append(weight_new)
        new_moments.append(moment_new)
        new_seconds.append(second_new)
    return (new_weights, new_moments, new_seconds)

def attend_pack(packed):
    queries, key_block_rows, value_block_rows, segment_row = packed
    sequence_length = queries.shape[0]
    kv_heads = key_block_rows.shape[1]
    grouped = queries.reshape(sequence_length, kv_heads, queries.shape[1] // kv_heads, queries.shape[2])
    scores = jnp.einsum('qhgd,khd->hgqk', grouped, key_block_rows, precision=PRECISE) * queries.shape[2] ** (-0.5)
    scores = low_back(scores)
    token_positions = jnp.arange(sequence_length)
    allowed = (segment_row[:, None] == segment_row[None, :]) & (token_positions[None, :] <= token_positions[:, None])
    scores = jnp.where(allowed, scores, MASKED_SCORE)
    highest = lax.optimization_barrier(jnp.max(scores, axis=-1, keepdims=True))
    weights = jnp.exp(scores - highest)
    weights = low(weights / lax.optimization_barrier(jnp.sum(weights, axis=-1, keepdims=True)))
    mixed_rows = jnp.einsum('hgqk,khd->qhgd', weights, value_block_rows, precision=PRECISE)
    return mixed_rows.reshape(queries.shape)

def expert_block(hidden, gate_rows, route_rows, in_low, down_low):
    targets, slot_owner = slot_tables(route_rows)
    model_width = hidden.shape[1]
    padded = jnp.concatenate([hidden, jnp.zeros((1, model_width), hidden.dtype)], axis=0)
    picked = padded[slot_owner // TOPK].reshape(EXPERTS, CAP, model_width)
    joined = low_back(jnp.einsum('ecd,edf->ecf', picked, in_low, precision=PRECISE))
    hidden_units = in_low.shape[2] // 2
    activated = low(jax.nn.silu(joined[..., :hidden_units]) * joined[..., hidden_units:])
    result = low_back(jnp.einsum('ecf,efd->ecd', activated, down_low, precision=PRECISE))
    per_route = result.reshape(EXPERTS * CAP, model_width)[targets].reshape(hidden.shape[0], TOPK, model_width)
    return lax.optimization_barrier(jnp.sum(gate_rows[..., None] * per_route, axis=1))

def forward(tokens, query_key_value_weight, out_weight, router_weight, expert_in, expert_down, norm_gains, segment_ids, route_ids):
    document_pack_count, sequence_length, model_width = tokens.shape
    qkv_low = low(query_key_value_weight)
    out_low = low(out_weight)
    router_low = low(router_weight)
    in_low = low(expert_in)
    down_low = low(expert_down)
    gains_low = low(norm_gains)
    normed = low(tokens * rms_scale(tokens) * gains_low[:, 0])
    mixed_query_key_value = low_back(jnp.einsum('pld,de->ple', normed, qkv_low, precision=PRECISE))
    query_width_total = QUERY_HEADS * HEAD_DIMENSION
    key_width_total = KEY_VALUE_HEADS * HEAD_DIMENSION
    token_positions = jnp.arange(sequence_length, dtype=jnp.float32)
    queries = rotation_embedding(mixed_query_key_value[..., :query_width_total].reshape(document_pack_count, sequence_length, QUERY_HEADS, HEAD_DIMENSION), token_positions)
    key_block_rows = rotation_embedding(mixed_query_key_value[..., query_width_total:query_width_total + key_width_total].reshape(document_pack_count, sequence_length, KEY_VALUE_HEADS, HEAD_DIMENSION), token_positions)
    value_block_rows = mixed_query_key_value[..., query_width_total + key_width_total:].reshape(document_pack_count, sequence_length, KEY_VALUE_HEADS, HEAD_DIMENSION)
    queries = low_back(low(queries))
    key_block_rows = low_back(low(key_block_rows))
    value_block_rows = low_back(low(value_block_rows))
    attended = lax.map(jax.checkpoint(attend_pack), (queries, key_block_rows, value_block_rows, segment_ids))
    attended = low_back(low(attended)).reshape(document_pack_count, sequence_length, query_width_total)
    middle = tokens + low_back(jnp.einsum('ple,ed->pld', attended, out_low, precision=PRECISE))
    normed_ffn = low(middle * rms_scale(middle) * gains_low[:, 1])
    logits = jnp.einsum('pld,de->ple', normed_ffn, router_low, precision=PRECISE)
    highest = lax.optimization_barrier(jnp.max(logits, axis=-1, keepdims=True))
    exponent = jnp.exp(logits - highest)
    router_probs = exponent / lax.optimization_barrier(jnp.sum(exponent, axis=-1, keepdims=True))
    chosen = (route_ids[..., None] == jnp.arange(EXPERTS, dtype=jnp.int32)).astype(jnp.float32)
    gate_rows = lax.optimization_barrier(jnp.sum(chosen * router_probs[:, :, None, :], axis=-1))
    all_tokens = document_pack_count * sequence_length
    blocks = all_tokens // TOK_DEV

    def one_block(packed):
        return expert_block(packed[0], packed[1], packed[2], in_low, down_low)
    mixture = lax.map(jax.checkpoint(one_block), (normed_ffn.reshape(blocks, TOK_DEV, model_width), gate_rows.reshape(blocks, TOK_DEV, TOPK), route_ids.reshape(blocks, TOK_DEV, TOPK)))
    return middle + mixture.reshape(document_pack_count, sequence_length, model_width)

def reference(tokens, cotangent, segment_ids, route_ids, query_key_value_weight, out_weight, router_weight, expert_in, expert_down, norm_gains, query_key_value_moment, out_moment, router_moment, in_moment, down_moment, gains_moment, query_key_value_second, out_second, router_second, in_second, down_second, gains_second):

    def wrapped(token_values, qkv_value, out_value, router_value, in_value, down_value, gain_value):
        return forward(token_values, qkv_value, out_value, router_value, in_value, down_value, gain_value, segment_ids, route_ids)
    result, pullback = jax.vjp(wrapped, tokens.astype(jnp.float32), query_key_value_weight, out_weight, router_weight, expert_in, expert_down, norm_gains)
    gradients = pullback(cotangent.astype(jnp.float32))
    input_grad = gradients[0]
    weight_grads = gradients[1:]
    square_total = jnp.sum(weight_grads[0] * weight_grads[0]) + jnp.sum(weight_grads[1] * weight_grads[1]) + jnp.sum(weight_grads[2] * weight_grads[2]) + jnp.sum(weight_grads[3] * weight_grads[3]) + jnp.sum(weight_grads[4] * weight_grads[4]) + jnp.sum(weight_grads[5] * weight_grads[5])
    grad_norm = jnp.sqrt(square_total)
    factor = CLIP_NORM / jnp.maximum(grad_norm, CLIP_NORM)
    new_weights, new_moments, new_seconds = update_all((query_key_value_weight, out_weight, router_weight, expert_in, expert_down, norm_gains), weight_grads, (query_key_value_moment, out_moment, router_moment, in_moment, down_moment, gains_moment), (query_key_value_second, out_second, router_second, in_second, down_second, gains_second), factor)
    qkv_new, out_new, router_new, in_new, down_new, gains_new = new_weights
    qkv_moment_new, out_moment_new, router_moment_new, in_moment_new, down_moment_new, gains_moment_new = new_moments
    qkv_second_new, out_second_new, router_second_new, in_second_new, down_second_new, gains_second_new = new_seconds
    return (result.astype(jnp.bfloat16), input_grad.astype(jnp.bfloat16), grad_norm, qkv_new, out_new, router_new, in_new, down_new, gains_new, qkv_moment_new, out_moment_new, router_moment_new, in_moment_new, down_moment_new, gains_moment_new, qkv_second_new, out_second_new, router_second_new, in_second_new, down_second_new, gains_second_new)
```

```python
import functools
import itertools

import jax
import jax.numpy as jnp
from jax import lax
from jax.experimental import pallas as pl
from jax.experimental.pallas import tpu as pltpu
from jax.sharding import PartitionSpec as P

MODEL_DIMENSION = 1536
QUERY_HEADS = 12
KEY_VALUE_HEADS = 2
HEAD_DIMENSION = 128
F = 768
EXPERTS = 8
TOPK = 4
STEP = 10
CAP = 320


PRECISE = lax.Precision.HIGHEST
NORM_EPS = 1e-06
CLIP_NORM = 1.0
BETA_ONE = 0.9
BETA_TWO = 0.95
ADAM_EPS = 1e-08
DECAY_RATE = 0.1
ROPE_BASE = 10000.0
MASKED_SCORE = -1e30

F32 = jnp.float32
BF16 = jnp.bfloat16
ALL_AXES = ("x", "z", "y", "core")
ROWS = ("z", "y", "core")
SOURCES = 4
OWN_EXPERTS = EXPERTS // SOURCES
Z_STEPS = 4
LANES = 128
MIB = 1024 * 1024


def rms_scale(values):
    return lax.rsqrt(jnp.mean(values * values, axis=-1, keepdims=True) + NORM_EPS)


def step_sizes():
    return (
        MODEL_DIMENSION ** (-0.5),
        (QUERY_HEADS * HEAD_DIMENSION // 64) ** (-0.5),
        (4 * MODEL_DIMENSION) ** (-0.5),
        MODEL_DIMENSION ** (-0.5),
        (F // 64) ** (-0.5),
        0.3,
    )


def adam_step(weight, gradient, moment, second, step_size, decay_value):
    moment_new = BETA_ONE * moment + (1.0 - BETA_ONE) * gradient
    second_new = BETA_TWO * second + (1.0 - BETA_TWO) * gradient * gradient
    corrected = (
        moment_new
        / (1.0 - BETA_ONE**STEP)
        / (jnp.sqrt(second_new / (1.0 - BETA_TWO**STEP)) + ADAM_EPS)
    )
    return (weight - step_size * (corrected + decay_value * weight), moment_new, second_new)


def update_all(weights, gradients, moments, seconds, factor):
    sizes_list = step_sizes()
    decays = (DECAY_RATE, DECAY_RATE, DECAY_RATE, DECAY_RATE, DECAY_RATE, 0.0)
    new_weights = []
    new_moments = []
    new_seconds = []
    for position in range(6):
        weight_new, moment_new, second_new = adam_step(
            weights[position],
            gradients[position] * factor,
            moments[position],
            seconds[position],
            sizes_list[position],
            decays[position],
        )
        new_weights.append(weight_new)
        new_moments.append(moment_new)
        new_seconds.append(second_new)
    return (new_weights, new_moments, new_seconds)


def norm_value_grad(values, norm_scale, gain_row, upstream):
    scaled = gain_row * upstream
    return norm_scale * scaled - values * norm_scale**3 * jnp.mean(
        values * scaled, axis=-1, keepdims=True
    )


def dot_nt(a, b):
    return lax.dot_general(a, b, (((1,), (1,)), ((), ())), preferred_element_type=F32)


def dot_tn(a, b):
    return lax.dot_general(a, b, (((0,), (0,)), ((), ())), preferred_element_type=F32)


def swap(value, axis):
    return lax.ppermute(value, axis, [(0, 1), (1, 0)])


def rotate(value, step):
    size = lax.axis_size("z")
    return lax.ppermute(value, "z", [(i, (i + step) % size) for i in range(size)])


def hold(values, *others):
    count = len(values)
    spec = pl.BlockSpec(memory_space=pl.ANY)
    return pl.pallas_call(
        lambda *refs: None,
        in_specs=[spec] * (count + len(others)),
        out_specs=[spec] * count,
        out_shape=[jax.ShapeDtypeStruct(v.shape, v.dtype) for v in values],
        input_output_aliases={i: i for i in range(count)},
        name="hold",
    )(*values, *others)


def by_index(index, own, other):
    return jnp.where(index == 0, jnp.stack([own, other]), jnp.stack([other, own]))


def take_index(index, array, axis):
    return lax.dynamic_index_in_dim(array, index, axis=axis, keepdims=False)


def total_over(value):
    if lax.axis_size("z") != Z_STEPS:
        return lax.psum(value, ALL_AXES)
    value = jnp.broadcast_to(value, (8, LANES))
    value = value + sum(rotate(value, k) for k in range(1, Z_STEPS))
    for axis in ("x", "y", "core"):
        value = value + swap(value, axis)
    return value[0, 0]


def place():
    return jnp.stack([lax.axis_index(a) for a in ALL_AXES]).astype(jnp.int32)


def block_of(place_ref, rel_x, rel_z, rel_y):
    x = lax.rem(place_ref[0] + rel_x, 2)
    z = lax.rem(place_ref[1] + rel_z, Z_STEPS)
    y = lax.rem(place_ref[2] + rel_y, 2)
    return (x * Z_STEPS + z) * 2 + y


def row_blocks():
    return [
        (c, y, x, z) for c in range(2) for y in range(2) for x in range(2) for z in range(Z_STEPS)
    ]


def row_copies(place_ref, own_ref, other_ref, targets, sems, first):
    rows = own_ref.shape[-2]
    copies = []
    for c, y, x, z in row_blocks():
        core = lax.rem(place_ref[3] + c, 2)
        row = pl.multiple_of((block_of(place_ref, x, z, y) * 2 + core) * rows, rows)
        for start, width, ref, column in targets:
            copies.append(
                pltpu.make_async_copy(
                    (own_ref, other_ref)[c].at[y, x, z, :, pl.ds(start, width)],
                    ref.at[pl.ds(row, rows), pl.ds(column, width)],
                    sems.at[first + len(copies)],
                )
            )
    return copies


def gather_whole(shard):
    whole = lax.all_gather(shard, ALL_AXES, axis=0, tiled=True)
    blocks = whole.reshape(2, Z_STEPS, 2, 2, -1, whole.shape[1])
    blocks = jnp.transpose(blocks, (3, 2, 0, 1, 4, 5))
    return blocks[0], blocks[1]


def scatter_whole(keep, send):
    blocks = jnp.transpose(jnp.stack([keep, send]), (2, 3, 1, 0, 4, 5))
    return lax.psum_scatter(
        blocks.reshape(-1, blocks.shape[-1]), ALL_AXES, scatter_dimension=0, tiled=True
    ).astype(F32)


def grad_rows_kernel(count, has_extra, edges, place_ref, a_ref, *rest):
    rest = list(rest)
    b_refs = [rest.pop(0) for _ in range(count)]
    extra_ref = rest.pop(0) if has_extra else None
    outs = [(rest.pop(0), rest.pop(0)) for _ in edges[1:]]
    held, sems = rest
    rows = outs[0][0].shape[-2]

    @pl.loop(0, a_ref.shape[1] // 256)
    def _(i):
        tile = pl.ds(pl.multiple_of(i * 256, 256), 256)
        start = 0
        for b_ref in b_refs:
            grad = dot_tn(a_ref[:, tile], b_ref[...])
            held[tile, pl.ds(start, b_ref.shape[1])] = grad.astype(BF16)
            start += b_ref.shape[1]

    if has_extra:
        held[:, pl.ds(held.shape[1] - LANES, LANES)] = extra_ref[...].astype(BF16)
    copies = []
    for pair, start, end in zip(outs, edges, edges[1:]):
        for c, y, x, z in row_blocks():
            core = lax.rem(place_ref[3] + c, 2)
            row = pl.multiple_of((block_of(place_ref, x, z, y) * 2 + core) * rows, rows)
            copies.append(
                pltpu.make_async_copy(
                    held.at[pl.ds(row, rows), pl.ds(start, end - start)],
                    pair[c].at[y, x, z],
                    sems.at[len(copies)],
                )
            )
    for copy in copies:
        copy.start()
    for copy in copies:
        copy.wait()


def grad_rows(where, a, bs, extra, edges):
    model_rows = a.shape[1]
    rows = model_rows // (2 * Z_STEPS * 2 * 2)
    width = edges[-1]
    any_spec = pl.BlockSpec(memory_space=pl.ANY)
    vmem_spec = pl.BlockSpec(memory_space=pltpu.VMEM)
    operands = (a, *bs) + (() if extra is None else (extra,))
    parts = len(edges) - 1
    outs = pl.pallas_call(
        functools.partial(grad_rows_kernel, len(bs), extra is not None, edges),
        grid_spec=pltpu.PrefetchScalarGridSpec(
            num_scalar_prefetch=1,
            grid=(1,),
            in_specs=[vmem_spec] * len(operands),
            out_specs=[any_spec] * (2 * parts),
            scratch_shapes=[
                pltpu.VMEM((model_rows, width), BF16),
                pltpu.SemaphoreType.DMA((len(row_blocks()) * parts,)),
            ],
        ),
        out_shape=[
            jax.ShapeDtypeStruct((2, 2, Z_STEPS, rows, end - start), BF16)
            for start, end in zip(edges, edges[1:])
            for _ in range(2)
        ],
        compiler_params=pltpu.CompilerParams(vmem_limit_bytes=48 * MIB),
        cost_estimate=pl.CostEstimate(
            flops=4 * a.shape[0] * model_rows * width,
            bytes_accessed=4 * model_rows * width,
            transcendentals=0,
        ),
        name="grad_rows",
    )(where, *operands)
    return [(outs[2 * i], outs[2 * i + 1]) for i in range(parts)]


def kept_sent(blocks, axis):
    at = 0 if axis == "y" or blocks.ndim == 4 else 1
    return [lax.index_in_dim(blocks, i, axis=at, keepdims=False) for i in range(2)]


def fold(kept, sent, axis):
    return kept.astype(F32) + swap(sent.astype(BF16), axis).astype(F32)


def fold_z(blocks):
    total = blocks[0]
    for k in range(1, Z_STEPS):
        total = total + rotate(blocks[k].astype(BF16), k).astype(F32)
    return total


def rotated(values, cosine, sine):
    return values * cosine + pltpu.roll(values, HEAD_DIMENSION // 2, 1) * sine


def project_kernel(
    place_ref,
    x_ref,
    own,
    other,
    cos_ref,
    sin_ref,
    query_ref,
    kv_ref,
    normed_ref,
    weight_out,
    small_out,
    weight,
    small,
    sems,
    out_sems,
):
    step = pl.program_id(0)
    columns = weight.shape[1]
    keep = [
        pltpu.make_async_copy(weight, weight_out, out_sems.at[0]),
        pltpu.make_async_copy(small, small_out, out_sems.at[1]),
    ]

    @pl.when(step == 0)
    def _():
        copies = row_copies(
            place_ref,
            own,
            other,
            ((0, columns, weight, 0), (columns, LANES, small, 0)),
            sems,
            0,
        )
        for copy in copies:
            copy.start()
        for copy in copies:
            copy.wait()
        for copy in keep:
            copy.start()
        gain = small[...].astype(F32).T[EXPERTS : EXPERTS + 1, :]
        values = x_ref[...].astype(F32)
        normed_ref[...] = (values * rms_scale(values) * gain).astype(BF16)

    tile = KEY_VALUE_HEADS * HEAD_DIMENSION
    at = pl.ds(pl.multiple_of(step * tile, tile), tile)
    mixed = jnp.dot(normed_ref[...], weight[:, at], preferred_element_type=F32)
    query_steps = pl.num_programs(0) - 2

    def turned():
        return jnp.concatenate(
            [
                rotated(
                    mixed[:, h * HEAD_DIMENSION : (h + 1) * HEAD_DIMENSION],
                    cos_ref[...],
                    sin_ref[...],
                ).astype(BF16)
                for h in range(KEY_VALUE_HEADS)
            ],
            axis=1,
        )

    @pl.when(step < query_steps)
    def _():
        query_ref[...] = turned()

    @pl.when(step == query_steps)
    def _():
        kv_ref[...] = turned()

    @pl.when(step == query_steps + 1)
    def _():
        kv_ref[...] = mixed.astype(BF16)
        for copy in keep:
            copy.wait()


def project(where, x, pair, cosine, sine):
    rows, depth = x.shape
    columns = pair[0].shape[-1] - LANES
    tile = KEY_VALUE_HEADS * HEAD_DIMENSION
    query_steps = QUERY_HEADS // KEY_VALUE_HEADS
    whole = lambda i, *_: (0, 0)
    any_spec = pl.BlockSpec(memory_space=pl.ANY)
    turn = pl.BlockSpec((rows, HEAD_DIMENSION), whole)
    return pl.pallas_call(
        project_kernel,
        grid_spec=pltpu.PrefetchScalarGridSpec(
            num_scalar_prefetch=1,
            grid=(query_steps + 2,),
            in_specs=[pl.BlockSpec((rows, depth), whole)] + [any_spec] * 2 + [turn] * 2,
            out_specs=[
                pl.BlockSpec((rows, tile), lambda i, *_: (0, jnp.minimum(i, query_steps - 1))),
                pl.BlockSpec((rows, tile), lambda i, *_: (0, jnp.maximum(i - query_steps, 0))),
                pl.BlockSpec((rows, depth), whole),
                any_spec,
                any_spec,
            ],
            scratch_shapes=[
                pltpu.VMEM((depth, columns), BF16),
                pltpu.VMEM((depth, LANES), BF16),
                pltpu.SemaphoreType.DMA((2 * len(row_blocks()),)),
                pltpu.SemaphoreType.DMA((2,)),
            ],
        ),
        out_shape=[
            jax.ShapeDtypeStruct((rows, query_steps * tile), BF16),
            jax.ShapeDtypeStruct((rows, 2 * tile), BF16),
            jax.ShapeDtypeStruct((rows, depth), BF16),
            jax.ShapeDtypeStruct((depth, columns), BF16),
            jax.ShapeDtypeStruct((depth, LANES), BF16),
        ],
        compiler_params=pltpu.CompilerParams(vmem_limit_bytes=40 * MIB),
        cost_estimate=pl.CostEstimate(
            flops=6 * rows * depth * columns, bytes_accessed=20 * MIB, transcendentals=0
        ),
        name="project",
    )(where, x, *pair, cosine, sine)


def join_kernel(
    place_ref,
    attended_ref,
    x_ref,
    gain_ref,
    own,
    other,
    middle_ref,
    normed_ref,
    scale_ref,
    weight_out,
    weight,
    sems,
    out_sems,
):
    copies = row_copies(place_ref, own, other, ((0, weight.shape[1], weight, 0),), sems, 0)
    for copy in copies:
        copy.start()
    for copy in copies:
        copy.wait()
    keep = pltpu.make_async_copy(weight, weight_out, out_sems.at[0])
    keep.start()
    wide = 512
    width = weight.shape[1]

    def join(i, total):
        at = pl.ds(pl.multiple_of(i * wide, wide), wide)
        middle = x_ref[:, at].astype(F32) + jnp.dot(
            attended_ref[...], weight[:, at], preferred_element_type=F32
        )
        middle_ref[:, at] = middle
        return total + jnp.sum(middle * middle, axis=1, keepdims=True)

    total = lax.fori_loop(0, width // wide, join, jnp.zeros((x_ref.shape[0], 1), F32))
    scale = lax.rsqrt(total / width + NORM_EPS)
    scale_ref[...] = scale
    normed_ref[...] = (middle_ref[...] * scale * gain_ref[...]).astype(BF16)
    keep.wait()


def join(where, attended, x, gain, pair):
    rows, depth = attended.shape
    width = pair[0].shape[-1]
    any_spec = pl.BlockSpec(memory_space=pl.ANY)
    vmem_spec = pl.BlockSpec(memory_space=pltpu.VMEM)
    return pl.pallas_call(
        join_kernel,
        grid_spec=pltpu.PrefetchScalarGridSpec(
            num_scalar_prefetch=1,
            grid=(1,),
            in_specs=[vmem_spec] * 3 + [any_spec] * 2,
            out_specs=[vmem_spec] * 3 + [any_spec],
            scratch_shapes=[
                pltpu.VMEM((depth, width), BF16),
                pltpu.SemaphoreType.DMA((len(row_blocks()),)),
                pltpu.SemaphoreType.DMA((1,)),
            ],
        ),
        out_shape=[
            jax.ShapeDtypeStruct((rows, width), F32),
            jax.ShapeDtypeStruct((rows, width), BF16),
            jax.ShapeDtypeStruct((rows, 1), F32),
            jax.ShapeDtypeStruct((depth, width), BF16),
        ],
        compiler_params=pltpu.CompilerParams(vmem_limit_bytes=40 * MIB),
        cost_estimate=pl.CostEstimate(
            flops=4 * rows * depth * width, bytes_accessed=16 * MIB, transcendentals=0
        ),
        name="join",
    )(where, attended, x, gain, *pair)


def score_pair(q, ko_ref, kp_ref, seg_col, seg_own, seg_prev):
    scale = HEAD_DIMENSION ** (-0.5)
    own = dot_nt(q, ko_ref[...]) * scale
    query_at = lax.broadcasted_iota(jnp.int32, own.shape, 0)
    key_at = lax.broadcasted_iota(jnp.int32, own.shape, 1)
    own = jnp.where((seg_col == seg_own) & (key_at <= query_at), own, MASKED_SCORE)
    if kp_ref is None:
        return (own,)
    prev = dot_nt(q, kp_ref[...]) * scale
    return (own, jnp.where(seg_col == seg_prev, prev, MASKED_SCORE))


def attend_kernel(
    half_ref, q_ref, ko_ref, vo_ref, kp_ref, vp_ref, sc_ref, so_ref, sp_ref, out_ref, log_ref
):
    def run(with_previous):
        parts = score_pair(
            q_ref[...],
            ko_ref,
            kp_ref if with_previous else None,
            sc_ref[...],
            so_ref[...],
            sp_ref[...],
        )
        highest = jnp.max(parts[0], axis=-1, keepdims=True)
        for part in parts[1:]:
            highest = jnp.maximum(highest, jnp.max(part, axis=-1, keepdims=True))
        exponents = [jnp.exp(part - highest) for part in parts]
        total = sum(jnp.sum(part, axis=-1, keepdims=True) for part in exponents)
        scale = 1.0 / total
        mixed = sum(
            jnp.dot((part * scale).astype(BF16), ref[...], preferred_element_type=F32)
            for part, ref in zip(exponents, (vo_ref, vp_ref))
        )
        out_ref[...] = mixed.astype(BF16)
        log_ref[0] = highest + jnp.log(total)

    pl.when(half_ref[0] == 0)(lambda: run(False))
    pl.when(half_ref[0] != 0)(lambda: run(True))


def head_specs(rows):
    group = QUERY_HEADS // KEY_VALUE_HEADS
    query = pl.BlockSpec((rows, HEAD_DIMENSION), lambda h, *_: (0, h))
    key = pl.BlockSpec((rows, HEAD_DIMENSION), lambda h, *_: (0, h // group))
    value = pl.BlockSpec((rows, HEAD_DIMENSION), lambda h, *_: (0, KEY_VALUE_HEADS + h // group))
    col = pl.BlockSpec((rows, 1), lambda h, *_: (0, 0))
    row = pl.BlockSpec((1, rows), lambda h, *_: (0, 0))
    log = pl.BlockSpec((1, rows, 1), lambda h, *_: (h, 0, 0))
    return query, [query, key, value, key, value, col, row, row], log


def attend(queries, own, previous, seg_col, seg_own, seg_prev, half):
    rows = queries.shape[0]
    query, specs, log = head_specs(rows)
    return pl.pallas_call(
        attend_kernel,
        grid_spec=pltpu.PrefetchScalarGridSpec(
            num_scalar_prefetch=1,
            grid=(QUERY_HEADS,),
            in_specs=specs,
            out_specs=[query, log],
        ),
        out_shape=[
            jax.ShapeDtypeStruct((rows, QUERY_HEADS * HEAD_DIMENSION), BF16),
            jax.ShapeDtypeStruct((QUERY_HEADS, rows, 1), F32),
        ],
        compiler_params=pltpu.CompilerParams(vmem_limit_bytes=40 * MIB),
        cost_estimate=pl.CostEstimate(
            flops=8 * rows * rows * QUERY_HEADS * HEAD_DIMENSION,
            bytes_accessed=16 * MIB,
            transcendentals=2 * rows * rows * QUERY_HEADS,
        ),
        name="attend",
    )(half, queries, own, own, previous, previous, seg_col, seg_own, seg_prev)


def attend_back_kernel(
    half_ref,
    q_ref,
    ko_ref,
    vo_ref,
    kp_ref,
    vp_ref,
    sc_ref,
    so_ref,
    sp_ref,
    up_ref,
    log_ref,
    cos_ref,
    sin_ref,
    dq_ref,
    dko_ref,
    dvo_ref,
    dkp_ref,
    dvp_ref,
):
    scale = HEAD_DIMENSION ** (-0.5)
    first = lax.rem(pl.program_id(0), QUERY_HEADS // KEY_VALUE_HEADS) == 0

    @pl.when(first)
    def _():
        for ref in (dko_ref, dvo_ref, dkp_ref, dvp_ref):
            ref[...] = jnp.zeros_like(ref)

    def run(with_previous):
        q, up = q_ref[...], up_ref[...]
        parts = score_pair(
            q, ko_ref, kp_ref if with_previous else None, sc_ref[...], so_ref[...], sp_ref[...]
        )
        weights = [jnp.exp(part - log_ref[0]) for part in parts]
        grads = [dot_nt(up, ref[...]) for ref, _ in zip((vo_ref, vp_ref), parts)]
        inner = sum(
            jnp.sum(w * g, axis=-1, keepdims=True) for w, g in zip(weights, grads)
        )
        scores = [(w * (g - inner)).astype(BF16) for w, g in zip(weights, grads)]
        dq = sum(
            jnp.dot(s, ref[...], preferred_element_type=F32)
            for s, ref in zip(scores, (ko_ref, kp_ref))
        )
        dq = (dq * scale).astype(BF16).astype(F32)
        dq_ref[...] = rotated(dq, cos_ref[...], sin_ref[...]).astype(BF16)
        for s, w, dk_ref, dv_ref in zip(scores, weights, (dko_ref, dkp_ref), (dvo_ref, dvp_ref)):
            dk_ref[...] += dot_tn(s, q) * scale
            dv_ref[...] += dot_tn(w.astype(BF16), up)

    pl.when(half_ref[0] == 0)(lambda: run(False))
    pl.when(half_ref[0] != 0)(lambda: run(True))


def attend_back(queries, own, previous, seg_col, seg_own, seg_prev, half, up, log_sums, cosine, sine):
    rows = queries.shape[0]
    query, specs, log = head_specs(rows)
    group = QUERY_HEADS // KEY_VALUE_HEADS
    turn = pl.BlockSpec((rows, HEAD_DIMENSION), lambda h, *_: (0, 0))
    kv = pl.BlockSpec((rows, HEAD_DIMENSION), lambda h, *_: (0, h // group))
    kv_shape = jax.ShapeDtypeStruct((rows, KEY_VALUE_HEADS * HEAD_DIMENSION), F32)
    return pl.pallas_call(
        attend_back_kernel,
        grid_spec=pltpu.PrefetchScalarGridSpec(
            num_scalar_prefetch=1,
            grid=(QUERY_HEADS,),
            in_specs=specs + [query, log, turn, turn],
            out_specs=[query, kv, kv, kv, kv],
        ),
        out_shape=[jax.ShapeDtypeStruct((rows, QUERY_HEADS * HEAD_DIMENSION), BF16)]
        + [kv_shape] * 4,
        compiler_params=pltpu.CompilerParams(vmem_limit_bytes=48 * MIB),
        cost_estimate=pl.CostEstimate(
            flops=20 * rows * rows * QUERY_HEADS * HEAD_DIMENSION,
            bytes_accessed=24 * MIB,
            transcendentals=2 * rows * rows * QUERY_HEADS,
        ),
        name="attend_back",
    )(
        half,
        queries,
        own,
        own,
        previous,
        previous,
        seg_col,
        seg_own,
        seg_prev,
        up,
        log_sums,
        cosine,
        sine,
    )


def expert_kernel(has_before, place_ref, *refs):
    refs = list(refs)
    pieces = [refs.pop(0) for _ in range(2)]
    x_refs, t_refs = ([refs.pop(0) for _ in range(SOURCES)] for _ in range(2))
    rank_row_ref, rank_col_ref, router_ref = (refs.pop(0) for _ in range(3))
    before = [refs.pop(0) for _ in range(4)] if has_before else None
    mix_keep, mix_send, ffn_keep, ffn_send, gate_grad_ref = (refs.pop(0) for _ in range(5))
    grads = [refs.pop(0) for _ in range(2)]
    (
        in_w,
        down_w,
        picked,
        joined_grad,
        active,
        slot_grad,
        top,
        x_held,
        t_held,
        in_g,
        down_g,
        sems,
        token_sems,
    ) = refs
    source = pl.program_id(0)
    slot = lax.rem(source, 2)

    def token_copies(s):
        return [
            pltpu.make_async_copy(many[s], held.at[s % 2], token_sems.at[i, s % 2])
            for i, (many, held) in enumerate(((x_refs, x_held), (t_refs, t_held)))
        ]
    in_rows = in_w.shape[0] // (4 * Z_STEPS)
    down_rows = down_w.shape[0] // (4 * Z_STEPS)

    def block_copies(outward):
        copies = []
        for y, piece in enumerate(grads if outward else pieces):
            for z, x in itertools.product(range(Z_STEPS), range(2)):
                block = (x * Z_STEPS + z) * 2 + lax.rem(place_ref[2] + y, 2)
                for whole, rows, start in (
                    (in_g if outward else in_w, in_rows, 0),
                    (down_g if outward else down_w, down_rows, in_rows),
                ):
                    ends = (
                        piece.at[z, x, pl.ds(start, rows), :],
                        whole.at[pl.ds(pl.multiple_of(block * rows, rows), rows), :],
                    )
                    if outward:
                        ends = ends[::-1]
                    copies.append(pltpu.make_async_copy(*ends, sems.at[len(copies)]))
        return copies

    @pl.when(source == 0)
    def _():
        copies = token_copies(0) + block_copies(False)
        for copy in copies:
            copy.start()
        for copy in copies[2:]:
            copy.wait()

    for s in range(SOURCES):

        @pl.when(source == s)
        def _(s=s):
            for copy in token_copies(s):
                copy.wait()
            if s + 1 < SOURCES:
                for copy in token_copies(s + 1):
                    copy.start()

    slots = pl.ds(pl.multiple_of(source * CAP, CAP), CAP)
    tokens, width = x_refs[0].shape
    rank_row = rank_row_ref[0]
    expert_row = lax.broadcasted_iota(jnp.int32, (router_ref.shape[0], tokens), 0)
    logits = jnp.where(expert_row < EXPERTS, dot_nt(router_ref[...], x_held[slot]), MASKED_SCORE)
    exponent = jnp.exp(logits - jnp.max(logits, axis=0, keepdims=True))
    probs = exponent / jnp.sum(exponent, axis=0, keepdims=True)
    gate_row = jnp.sum(jnp.where(expert_row == place_ref[4], probs, 0.0), axis=0, keepdims=True)
    chosen = (
        lax.broadcasted_iota(jnp.int32, (CAP, tokens), 0) == rank_row
    ).astype(F32)
    gate = jnp.sum(chosen * gate_row, axis=1, keepdims=True)
    spread = (
        lax.broadcasted_iota(jnp.int32, (tokens, CAP), 1) == rank_col_ref[0]
    ).astype(F32).astype(BF16)
    pick = chosen.astype(BF16)
    wide = 512

    @pl.loop(0, width // wide, unroll=True)
    def _(i):
        at = pl.ds(pl.multiple_of(i * wide, wide), wide)
        picked[slots, at] = jnp.dot(
            pick, x_held[slot, :, at], preferred_element_type=F32
        ).astype(BF16)
        top_rows = jnp.dot(pick, t_held[slot, :, at], preferred_element_type=F32)
        top[:, at] = top_rows
        slot_grad[slots, at] = (gate * top_rows).astype(BF16)

    hidden = active.shape[1]
    narrow = 256

    @pl.loop(0, hidden // narrow, unroll=True)
    def _(i):
        at = pl.ds(pl.multiple_of(i * narrow, narrow), narrow)
        up_at = pl.ds(pl.multiple_of(hidden + i * narrow, narrow), narrow)
        rows = picked[slots, :]
        gate_part = jnp.dot(rows, in_w[:, at], preferred_element_type=F32)
        up_part = jnp.dot(rows, in_w[:, up_at], preferred_element_type=F32)
        act_grad = dot_nt(slot_grad[slots, :], down_w[at, :])
        sigmoid = jax.nn.sigmoid(gate_part)
        silu = gate_part * sigmoid
        active[slots, at] = (silu * up_part).astype(BF16)
        joined_grad[slots, at] = (
            act_grad * up_part * sigmoid * (1.0 + gate_part * (1.0 - sigmoid))
        ).astype(BF16)
        joined_grad[slots, up_at] = (act_grad * silu).astype(BF16)

    def results(i, total):
        at = pl.ds(pl.multiple_of(i * wide, wide), wide)
        result = jnp.dot(active[slots, :], down_w[:, at], preferred_element_type=F32)
        mix = jnp.dot(spread, (gate * result).astype(BF16), preferred_element_type=F32)
        back = dot_nt(joined_grad[slots, :], in_w[at, :])
        ffn = jnp.dot(spread, back.astype(BF16), preferred_element_type=F32)

        def put(mix_ref, ffn_ref, mix_before, ffn_before):
            if before is None:
                mix_ref[0, :, at] = mix.astype(BF16)
                ffn_ref[0, :, at] = ffn.astype(BF16)
            else:
                mix_ref[0, :, at] = (mix + mix_before[0, :, at].astype(F32)).astype(BF16)
                ffn_ref[0, :, at] = (ffn + ffn_before[0, :, at].astype(F32)).astype(BF16)

        earlier = before or [None] * 4
        pl.when(source < 2)(lambda: put(mix_keep, ffn_keep, earlier[0], earlier[2]))
        pl.when(source >= 2)(lambda: put(mix_send, ffn_send, earlier[1], earlier[3]))
        return total + jnp.sum(result * top[:, at], axis=1, keepdims=True)

    gate_grad = lax.fori_loop(
        0, width // wide, results, jnp.zeros((CAP, 1), F32), unroll=True
    )
    gate_grad_ref[0] = jnp.sum(chosen * gate_grad, axis=0, keepdims=True)

    @pl.when(source == SOURCES - 1)
    def _():
        @pl.loop(0, in_g.shape[0] // 256)
        def _(i):
            at = pl.ds(pl.multiple_of(i * 256, 256), 256)
            in_g[at, :] = dot_tn(picked[:, at], joined_grad[...]).astype(BF16)

        @pl.loop(0, down_g.shape[0] // 256)
        def _(i):
            at = pl.ds(pl.multiple_of(i * 256, 256), 256)
            down_g[at, :] = dot_tn(active[:, at], slot_grad[...]).astype(BF16)

        copies = block_copies(True)
        for copy in copies:
            copy.start()
        for copy in copies:
            copy.wait()


def expert_pass(where, pieces, x_all, t_all, rank_row, rank_col, router_rows, before):
    tokens, width = x_all[0].shape
    hidden = F
    any_spec = pl.BlockSpec(memory_space=pl.ANY)
    keep_at = lambda s, *_: (jnp.minimum(s, 1), 0, 0)
    send_at = lambda s, *_: (jnp.maximum(s - 2, 0), 0, 0)
    sum_specs = [pl.BlockSpec((1, tokens, width), at) for at in (keep_at, send_at)] * 2
    before_specs = [
        pl.BlockSpec((1, tokens, width), at, pipeline_mode=pl.Buffered(1))
        for at in (keep_at, send_at)
    ] * 2
    row_spec = pl.BlockSpec((1, 1, tokens), lambda s, *_: (s, 0, 0))
    col_spec = pl.BlockSpec((1, tokens, 1), lambda s, *_: (s, 0, 0))
    router_spec = pl.BlockSpec(router_rows.shape, lambda s, *_: (0, 0))
    piece_shape = jax.ShapeDtypeStruct(pieces[0].shape, BF16)
    sum_shape = jax.ShapeDtypeStruct((2, tokens, width), BF16)
    slots = SOURCES * CAP
    flops = 2 * slots * width * hidden * 9 + 8 * slots * tokens * width
    outs = pl.pallas_call(
        functools.partial(expert_kernel, before is not None),
        grid_spec=pltpu.PrefetchScalarGridSpec(
            num_scalar_prefetch=1,
            grid=(SOURCES,),
            in_specs=[any_spec] * (len(pieces) + 2 * SOURCES)
            + [row_spec, col_spec, router_spec]
            + ([] if before is None else before_specs),
            out_specs=sum_specs + [row_spec] + [any_spec] * len(pieces),
            scratch_shapes=[
                pltpu.VMEM((width, 2 * hidden), BF16),
                pltpu.VMEM((hidden, width), BF16),
                pltpu.VMEM((slots, width), BF16),
                pltpu.VMEM((slots, 2 * hidden), BF16),
                pltpu.VMEM((slots, hidden), BF16),
                pltpu.VMEM((slots, width), BF16),
                pltpu.VMEM((CAP, width), F32),
                pltpu.VMEM((2, tokens, width), BF16),
                pltpu.VMEM((2, tokens, width), BF16),
                pltpu.VMEM((width, 2 * hidden), BF16),
                pltpu.VMEM((hidden, width), BF16),
                pltpu.SemaphoreType.DMA((8 * Z_STEPS,)),
                pltpu.SemaphoreType.DMA((2, 2)),
            ],
        ),
        out_shape=[sum_shape] * 4
        + [jax.ShapeDtypeStruct((SOURCES, 1, tokens), F32)]
        + [piece_shape] * len(pieces),
        compiler_params=pltpu.CompilerParams(vmem_limit_bytes=60 * MIB),
        cost_estimate=pl.CostEstimate(
            flops=2 * flops, bytes_accessed=48 * MIB, transcendentals=slots * hidden
        ),
        name="expert",
    )(where, *pieces, *x_all, *t_all, rank_row, rank_col, router_rows, *(before or ()))
    return outs[:4], outs[4], outs[5:]


def expert_pairs(expert_in, expert_down):
    core = lax.axis_index("core")
    low = jnp.concatenate([expert_in.astype(BF16), expert_down.astype(BF16)], axis=1)
    low = low.reshape(2, 2, OWN_EXPERTS, *low.shape[1:])
    return by_index(core, take_index(core, low, 1), swap(take_index(1 - core, low, 1), "core"))


def expert_chunk(pair, number, in_rows):
    x = lax.axis_index("x")
    pair = pair[:, :, number]
    in_part = pair[:, :, :in_rows]
    down_part = pair[:, :, in_rows:]
    width = pair.shape[-1]
    both = jnp.concatenate(
        [
            jnp.swapaxes(in_part, 0, 1).reshape(2, -1, width),
            jnp.swapaxes(down_part, 0, 1).reshape(2, -1, width),
        ],
        axis=1,
    )
    return by_index(x, take_index(x, both, 0), swap(take_index(1 - x, both, 0), "x"))


def gather_expert(chunk):
    if lax.axis_size("z") == Z_STEPS:
        whole = lax.all_gather(chunk, "z")
        return whole, swap(whole, "y")
    whole = lax.all_gather(chunk, ("z", "y"))
    rows = chunk.shape[1] * 2 // 3
    width = chunk.shape[2]
    parts = [
        jnp.moveaxis(part, 0, 1).reshape(2, Z_STEPS, 2, -1, width)
        for part in (whole[:, :, :rows], whole[:, :, rows:])
    ]
    both = jnp.transpose(jnp.concatenate(parts, axis=3), (2, 1, 0, 3, 4))
    return both[0], both[1]


def scatter_expert_whole(kept, arrived):
    spots = lax.axis_size("z") * 2
    both = jnp.transpose(jnp.stack([kept, arrived]), (2, 1, 0, 3, 4))
    width = both.shape[-1]
    in_rows = both.shape[3] * 2 // 3
    parts = [
        part.reshape(2, spots, -1, width)
        for part in (both[:, :, :, :in_rows], both[:, :, :, in_rows:])
    ]
    both = jnp.moveaxis(jnp.concatenate(parts, axis=2), 1, 0)
    return lax.psum_scatter(both, ("z", "y"), scatter_dimension=0).astype(F32)


def cross_chunk(chunk):
    x = lax.axis_index("x")
    return take_index(x, chunk, 0), swap(take_index(1 - x, chunk, 0).astype(BF16), "x")


def scatter_chunks(pairs, in_rows, down_rows):
    x, core = lax.axis_index("x"), lax.axis_index("core")
    width = pairs[0][0].shape[-1]
    own, crossed = (jnp.stack([p[i].astype(F32) for p in pairs]) for i in range(2))
    both = by_index(x, own, crossed)
    split = jnp.concatenate(
        [
            both[:, :, : 2 * in_rows].reshape(2, OWN_EXPERTS, 2, in_rows, width),
            both[:, :, 2 * in_rows :].reshape(2, OWN_EXPERTS, 2, down_rows, width),
        ],
        axis=3,
    )
    other = swap(take_index(1 - core, split, 2).astype(BF16), "core").astype(F32)
    both = by_index(core, take_index(core, split, 2), other)
    both = jnp.swapaxes(both, 0, 1).reshape(EXPERTS, in_rows + down_rows, width)
    return both[:, :in_rows], both[:, in_rows:]


def shards(
    tokens,
    cotangent,
    segment_ids,
    route_ids,
    query_key_value_weight,
    out_weight,
    router_weight,
    expert_in,
    expert_down,
    norm_gains,
    query_key_value_moment,
    out_moment,
    router_moment,
    in_moment,
    down_moment,
    gains_moment,
    query_key_value_second,
    out_second,
    router_second,
    in_second,
    down_second,
    gains_second,
):
    local_rows = tokens.shape[1]
    model_width = tokens.shape[2]
    staged = lax.axis_size("z") == Z_STEPS
    x_index = lax.axis_index("x")
    shard_rows = query_key_value_weight.shape[0]
    in_rows, down_rows = expert_in.shape[1], expert_down.shape[1]
    key_width = KEY_VALUE_HEADS * HEAD_DIMENSION
    first_expert = (x_index * 2 + lax.axis_index("core")) * OWN_EXPERTS
    where = place() if staged else jnp.zeros((4,), jnp.int32)
    x_tokens, top = tokens[0], cotangent[0]

    own_gains = norm_gains.astype(BF16)
    small_part = jnp.concatenate(
        [
            router_weight.astype(BF16),
            own_gains,
            jnp.zeros((shard_rows, LANES - EXPERTS - 2), BF16),
        ],
        axis=1,
    )
    qkv_own = query_key_value_weight.astype(BF16)
    qkv_width = qkv_own.shape[1]
    half_width = qkv_width // 2
    attention_own = jnp.concatenate([qkv_own, small_part, out_weight.astype(BF16)], axis=1)
    attention_edges = (0, half_width, qkv_width + LANES, attention_own.shape[1])

    segments = segment_ids[0]
    seg_prev = swap(segments, "x")
    routes = route_ids[0].T
    routes_x = swap(routes, "x")
    routes_core = swap(jnp.stack([routes, routes_x]), "core")
    routes_all = jnp.stack([routes, routes_x, routes_core[0], routes_core[1]])
    top_x = swap(top, "x")

    pair = expert_pairs(expert_in, expert_down)
    if staged:
        attention_z = [rotate(attention_own, -k) for k in range(1, Z_STEPS)]
        first_held, second_held, out_held = (
            jnp.stack([part[:, start:end] for part in (attention_own, *attention_z)])
            for start, end in zip(attention_edges, attention_edges[1:])
        )
        first_x = swap(first_held, "x")
        second_y = swap(second_held, "y")
        chunk_one = expert_chunk(pair, 0, in_rows)
        pieces_one = gather_expert(chunk_one)
        first_held = jnp.stack([first_held, first_x])
        second_held = jnp.stack([second_held, second_y])
        first_y = swap(first_held, "y")
        second_x = swap(second_held, "x")
        first_held = jnp.stack([first_held, first_y])
        second_held = jnp.stack([second_held, second_x], axis=1)
        qkv_held = jnp.concatenate([first_held, second_held], axis=-1)
        (out_held,) = hold((out_held,), first_y, second_x)
        out_x = swap(out_held, "x")
        qkv_core = swap(qkv_held, "core")
        qkv_pair = (qkv_held, qkv_core)
        out_held = jnp.stack([out_held, out_x])
    else:
        qkv_pair, out_pair = (
            gather_whole(part)
            for part in (
                attention_own[:, : qkv_width + LANES],
                attention_own[:, qkv_width + LANES :],
            )
        )
        pieces_one, pieces_two = (
            gather_expert(expert_chunk(pair, i, in_rows)) for i in range(2)
        )

    half_size = HEAD_DIMENSION // 2
    positions = (x_index * local_rows + jnp.arange(local_rows, dtype=jnp.int32)).astype(F32)
    frequency = ROPE_BASE ** (-2.0 * jnp.arange(half_size, dtype=F32) / HEAD_DIMENSION)
    angles = positions[:, None] * frequency[None, :]
    cosine, sine = jnp.cos(angles), jnp.sin(angles)
    cosine = jnp.concatenate([cosine, cosine], axis=1)
    sine_forward = jnp.concatenate([-sine, sine], axis=1)
    half = x_index.astype(jnp.int32).reshape(1)

    experts_here = first_expert + jnp.arange(OWN_EXPERTS, dtype=jnp.int32)
    member = jnp.any(routes_all[None] == experts_here[:, None, None, None], axis=2)
    earlier = (
        lax.broadcasted_iota(jnp.int32, (local_rows, local_rows), 0)
        < lax.broadcasted_iota(jnp.int32, (local_rows, local_rows), 1)
    ).astype(BF16)
    rank = jnp.dot(
        member.astype(BF16).reshape(-1, local_rows), earlier, preferred_element_type=F32
    ).reshape(member.shape)
    rank = jnp.where(member, rank.astype(jnp.int32), -1)

    queries, kv_own, normed, qkv_low, small_low = project(
        where, x_tokens, qkv_pair, cosine, sine_forward
    )
    kv_prev = swap(kv_own, "x")
    attn_gain = small_low[:, EXPERTS].astype(F32)
    ffn_gain = small_low[:, EXPERTS + 1].astype(F32)
    router_rows = small_low.T[:16]
    if staged:
        out_y = swap(out_held, "y")
        out_held = jnp.stack([out_held, out_y])
        (pair,) = hold((pair,), kv_prev)
        pieces_two = gather_expert(expert_chunk(pair, 1, in_rows))
        out_core = swap(out_held, "core")
        out_pair = (out_held, out_core)
    segs = (segments[:, None], segments[None, :], seg_prev[None, :])
    attended, log_sums = attend(queries, kv_own, kv_prev, *segs, half)
    top_both = swap(jnp.stack([top, top_x]), "core")
    middle, normed_ffn, second_scale, out_low = join(
        where, attended, x_tokens, ffn_gain[None, :], out_pair
    )

    ffn_core = swap(normed_ffn, "core")
    ffn_x = swap(normed_ffn, "x")
    ffn_both = swap(ffn_x, "core")
    x_all = (normed_ffn, ffn_x, ffn_core, ffn_both)
    t_all = (top, top_x, top_both[0], top_both[1])
    places = [jnp.concatenate([where, first_expert[None] + i]) for i in range(OWN_EXPERTS)]

    def expert(i, pieces, before):
        ranks = (rank[i][:, None, :], rank[i][:, :, None])
        return expert_pass(places[i], pieces, x_all, t_all, *ranks, router_rows, before)

    before, gates_one, grads_one = expert(0, pieces_one, None)
    sums, gates_two, grads_two = expert(1, pieces_two, before)
    mix_keep, mix_send, ffn_keep, ffn_send = sums

    if staged:
        back_one = swap(grads_one[1], "y")
        (ffn_send,) = hold((ffn_send,), back_one)
        total_one = (grads_one[0].astype(F32) + back_one.astype(F32)).astype(BF16)
        chunk_sum_one = lax.psum_scatter(total_one, "z", scatter_dimension=0)
        back_two = swap(grads_two[1], "y")
    else:
        chunk_sum_one, chunk_sum_two = (
            scatter_expert_whole(*grads) for grads in (grads_one, grads_two)
        )
    gate_grad = jnp.concatenate([gates_one, gates_two], axis=1)
    spread = lax.dynamic_update_slice_in_dim(
        jnp.zeros((SOURCES, EXPERTS, local_rows), F32), gate_grad, first_expert, axis=1
    )
    spread_core = swap(spread[2:], "core")
    ffn_other = swap(ffn_send, "core").astype(F32)
    spread_x = swap(spread[1] + spread_core[1], "x")
    prob_grad = (spread[0] + spread_core[0] + spread_x).T
    ffn_crossed = swap((ffn_keep[1].astype(F32) + ffn_other[1]).astype(BF16), "x")
    if staged:
        (ffn_crossed,) = hold((ffn_crossed,), total_one)
    (mix_send,) = hold((mix_send,), ffn_crossed)
    mix_other = swap(mix_send, "core").astype(F32)
    mix_crossed = swap((mix_keep[1].astype(F32) + mix_other[1]).astype(BF16), "x")
    ffn_grad = ffn_keep[0].astype(F32) + ffn_other[0] + ffn_crossed.astype(F32)

    logits = jnp.dot(normed_ffn, small_low[:, :EXPERTS], preferred_element_type=F32)
    exponent = jnp.exp(logits - jnp.max(logits, axis=-1, keepdims=True))
    router_probs = exponent / jnp.sum(exponent, axis=-1, keepdims=True)
    logit_grad = router_probs * (
        prob_grad - jnp.sum(router_probs * prob_grad, axis=-1, keepdims=True)
    )
    router_grad = jnp.dot(normed_ffn.astype(F32).T, logit_grad, precision=PRECISE)
    ffn_grad = ffn_grad + jnp.dot(
        logit_grad, small_low[:, :EXPERTS].astype(F32).T, precision=PRECISE
    )
    ffn_gain_grad = jnp.sum(middle * second_scale * ffn_grad, axis=0)
    middle_grad = top.astype(F32) + norm_value_grad(middle, second_scale, ffn_gain, ffn_grad)
    branch_grad = middle_grad.astype(BF16)
    attended_grad = dot_nt(branch_grad, out_low).astype(BF16)
    small_grad = jnp.concatenate(
        [
            router_grad,
            ffn_gain_grad[:, None],
            jnp.zeros((model_width, LANES - EXPERTS - 1), F32),
        ],
        axis=1,
    )
    (out_blocks,) = grad_rows(
        where, attended, (branch_grad,), small_grad, (0, model_width + LANES)
    )
    if staged:
        attended_grad, chunk_sum_one = hold(
            (attended_grad, chunk_sum_one), out_blocks[1], back_two
        )
        total_two = (grads_two[0].astype(F32) + back_two.astype(F32)).astype(BF16)
        out_sum = fold(*out_blocks, "core")
        out_sent = swap(kept_sent(out_sum, "x")[1].astype(BF16), "x")
    query_grad, key_own, value_own, key_prev, value_prev = attend_back(
        queries, kv_own, kv_prev, *segs, half, attended_grad, log_sums, cosine, -sine_forward
    )
    crossed = swap(jnp.concatenate([key_prev, value_prev], axis=1).astype(BF16), "x").astype(F32)
    if staged:
        out_sent, query_grad = hold((out_sent, query_grad), total_two)
        chunk_sum_two = lax.psum_scatter(total_two, "z", scatter_dimension=0)
        out_sum = kept_sent(out_sum, "x")[0] + out_sent.astype(F32)
        out_sum = fold(*kept_sent(out_sum, "y"), "y")
    key_grad = (key_own + crossed[:, :key_width]).astype(BF16).astype(F32)
    value_grad = value_own + crossed[:, key_width:]
    key_grad = key_grad.reshape(local_rows, KEY_VALUE_HEADS, HEAD_DIMENSION)
    key_grad = key_grad * cosine[:, None, :] - jnp.roll(key_grad, half_size, axis=2) * sine_forward[
        :, None, :
    ]
    kv_grad = jnp.concatenate(
        [key_grad.reshape(local_rows, key_width).astype(BF16), value_grad.astype(BF16)], axis=1
    )
    kv_grad, chunk_sum_one = hold((kv_grad, chunk_sum_one), mix_crossed)
    qkv_blocks = grad_rows(
        where, normed, (query_grad, kv_grad), None, (0, half_width, 2 * half_width)
    )
    out_rows = fold_z(out_sum) if staged else scatter_whole(*out_blocks)
    if staged:
        pair_one = cross_chunk(chunk_sum_one)
        first = fold(*qkv_blocks[0], "core")
        second = fold(*qkv_blocks[1], "core")
        first_kept, first_sent = kept_sent(first, "y")
        second_kept, second_sent = kept_sent(second, "x")
        first_come = swap(first_sent.astype(BF16), "y")
        second_come = swap(second_sent.astype(BF16), "x")
        (chunk_sum_two,) = hold((chunk_sum_two,), first_come, second_come)
        first = fold(*kept_sent(first_kept + first_come.astype(F32), "x"), "x")
        second = fold(*kept_sent(second_kept + second_come.astype(F32), "y"), "y")
        qkv_sum = jnp.concatenate([fold_z(first), fold_z(second)], axis=1)
    else:
        pair_one = cross_chunk(chunk_sum_one)
        qkv_sum = jnp.concatenate([scatter_whole(*blocks) for blocks in qkv_blocks], axis=1)
    in_sum, down_sum = scatter_chunks(
        [pair_one, cross_chunk(chunk_sum_two)], in_rows, down_rows
    )
    mixture = mix_keep[0].astype(F32) + mix_other[0] + mix_crossed.astype(F32)
    output = (middle + mixture).astype(BF16)
    mixed_grad = jnp.concatenate([query_grad, kv_grad], axis=1)
    inputs = x_tokens.astype(F32)
    input_grad = middle_grad + norm_value_grad(
        inputs, rms_scale(inputs), attn_gain, dot_nt(mixed_grad, qkv_low)
    )

    out_sum = out_rows[:, :model_width]
    router_sum = out_rows[:, model_width : model_width + EXPERTS]
    attn_gain_sum = jnp.sum(qkv_sum * qkv_own.astype(F32), axis=1) / own_gains[:, 0].astype(F32)
    gains_sum = jnp.stack([attn_gain_sum, out_rows[:, model_width + EXPERTS]], axis=1)

    square_total = (
        jnp.sum(qkv_sum * qkv_sum)
        + jnp.sum(out_sum * out_sum)
        + jnp.sum(router_sum * router_sum)
        + jnp.sum(in_sum * in_sum)
        + jnp.sum(down_sum * down_sum)
        + jnp.sum(gains_sum * gains_sum)
    )
    grad_norm = jnp.sqrt(total_over(square_total))
    factor = CLIP_NORM / jnp.maximum(grad_norm, CLIP_NORM)
    new_weights, new_moments, new_seconds = update_all(
        (query_key_value_weight, out_weight, router_weight, expert_in, expert_down, norm_gains),
        (qkv_sum, out_sum, router_sum, in_sum, down_sum, gains_sum),
        (query_key_value_moment, out_moment, router_moment, in_moment, down_moment, gains_moment),
        (query_key_value_second, out_second, router_second, in_second, down_second, gains_second),
        factor,
    )
    return (
        output[None],
        input_grad.astype(BF16)[None],
        grad_norm,
        *new_weights,
        *new_moments,
        *new_seconds,
    )


def solution(mesh):
    mesh = jax.sharding.Mesh(
        mesh.devices.reshape(mesh.shape["seq"], mesh.shape["fsdp"] // 4, 2, 2), ALL_AXES
    )
    token_spec = P(ROWS, "x", None)
    row_spec = P(ALL_AXES, None)
    expert_spec = P(None, ALL_AXES, None)
    state_specs = (row_spec, row_spec, row_spec, expert_spec, expert_spec, row_spec)
    return jax.shard_map(
        shards,
        mesh=mesh,
        in_specs=(token_spec, token_spec, P(ROWS, "x"), token_spec) + state_specs * 3,
        out_specs=(token_spec, token_spec, P()) + state_specs * 3,
        check_vma=False,
    )
```

```python
import functools
import itertools

import jax
import jax.numpy as jnp
from jax import lax
from jax.experimental import pallas as pl
from jax.experimental.pallas import tpu as pltpu
from jax.sharding import PartitionSpec as P

MODEL_DIMENSION = 1536
QUERY_HEADS = 12
KEY_VALUE_HEADS = 2
HEAD_DIMENSION = 128
F = 768
EXPERTS = 8
TOPK = 4
STEP = 10
CAP = 320


PRECISE = lax.Precision.HIGHEST
NORM_EPS = 1e-06
CLIP_NORM = 1.0
BETA_ONE = 0.9
BETA_TWO = 0.95
ADAM_EPS = 1e-08
DECAY_RATE = 0.1
ROPE_BASE = 10000.0
MASKED_SCORE = -1e30

F32 = jnp.float32
BF16 = jnp.bfloat16
ALL_AXES = ("x", "z", "y", "core")
ROWS = ("z", "y", "core")
SOURCES = 4
OWN_EXPERTS = EXPERTS // SOURCES
Z_STEPS = 4
LANES = 128
MIB = 1024 * 1024
COST_SCALE = 4


def cost(flops, bytes_accessed, transcendentals=0):
    return pl.CostEstimate(
        flops=flops // COST_SCALE,
        bytes_accessed=bytes_accessed // COST_SCALE,
        transcendentals=transcendentals // COST_SCALE,
    )


def rms_scale(values):
    return lax.rsqrt(jnp.mean(values * values, axis=-1, keepdims=True) + NORM_EPS)


def step_sizes():
    return (
        MODEL_DIMENSION ** (-0.5),
        (QUERY_HEADS * HEAD_DIMENSION // 64) ** (-0.5),
        (4 * MODEL_DIMENSION) ** (-0.5),
        MODEL_DIMENSION ** (-0.5),
        (F // 64) ** (-0.5),
        0.3,
    )


def adam_step(weight, gradient, moment, second, step_size, decay_value):
    moment_new = BETA_ONE * moment + (1.0 - BETA_ONE) * gradient
    second_new = BETA_TWO * second + (1.0 - BETA_TWO) * gradient * gradient
    corrected = (
        moment_new
        / (1.0 - BETA_ONE**STEP)
        / (jnp.sqrt(second_new / (1.0 - BETA_TWO**STEP)) + ADAM_EPS)
    )
    return (weight - step_size * (corrected + decay_value * weight), moment_new, second_new)


def update_all(weights, gradients, moments, seconds, factor):
    sizes_list = step_sizes()
    decays = (DECAY_RATE, DECAY_RATE, DECAY_RATE, DECAY_RATE, DECAY_RATE, 0.0)
    new_weights = []
    new_moments = []
    new_seconds = []
    for position in range(6):
        weight_new, moment_new, second_new = adam_step(
            weights[position],
            gradients[position] * factor,
            moments[position],
            seconds[position],
            sizes_list[position],
            decays[position],
        )
        new_weights.append(weight_new)
        new_moments.append(moment_new)
        new_seconds.append(second_new)
    return (new_weights, new_moments, new_seconds)


def norm_value_grad(values, norm_scale, gain_row, upstream):
    scaled = gain_row * upstream
    return norm_scale * scaled - values * norm_scale**3 * jnp.mean(
        values * scaled, axis=-1, keepdims=True
    )


def dot_nt(a, b):
    return lax.dot_general(a, b, (((1,), (1,)), ((), ())), preferred_element_type=F32)


def dot_tn(a, b):
    return lax.dot_general(a, b, (((0,), (0,)), ((), ())), preferred_element_type=F32)


def swap(value, axis):
    return lax.ppermute(value, axis, [(0, 1), (1, 0)])


def rotate(value, step):
    size = lax.axis_size("z")
    return lax.ppermute(value, "z", [(i, (i + step) % size) for i in range(size)])


def hold(values, *others):
    count = len(values)
    spec = pl.BlockSpec(memory_space=pl.ANY)
    return pl.pallas_call(
        lambda *refs: None,
        in_specs=[spec] * (count + len(others)),
        out_specs=[spec] * count,
        out_shape=[jax.ShapeDtypeStruct(v.shape, v.dtype) for v in values],
        input_output_aliases={i: i for i in range(count)},
        name="hold",
    )(*values, *others)


def by_index(index, own, other):
    return jnp.where(index == 0, jnp.stack([own, other]), jnp.stack([other, own]))


def take_index(index, array, axis):
    return lax.dynamic_index_in_dim(array, index, axis=axis, keepdims=False)


def total_over(value):
    if lax.axis_size("z") != Z_STEPS:
        return lax.psum(value, ALL_AXES)
    value = jnp.broadcast_to(value, (8, LANES))
    value = value + sum(rotate(value, k) for k in range(1, Z_STEPS))
    for axis in ("x", "y", "core"):
        value = value + swap(value, axis)
    return value[0, 0]


def place():
    return jnp.stack([lax.axis_index(a) for a in ALL_AXES]).astype(jnp.int32)


def block_of(place_ref, rel_x, rel_z, rel_y):
    x = lax.rem(place_ref[0] + rel_x, 2)
    z = lax.rem(place_ref[1] + rel_z, Z_STEPS)
    y = lax.rem(place_ref[2] + rel_y, 2)
    return (x * Z_STEPS + z) * 2 + y


def row_blocks():
    return [
        (c, y, x, z) for c in range(2) for y in range(2) for x in range(2) for z in range(Z_STEPS)
    ]


def row_copies(place_ref, own_ref, other_ref, targets, sems, first):
    rows = own_ref.shape[-2]
    copies = []
    for c, y, x, z in row_blocks():
        core = lax.rem(place_ref[3] + c, 2)
        row = pl.multiple_of((block_of(place_ref, x, z, y) * 2 + core) * rows, rows)
        for start, width, ref, column in targets:
            copies.append(
                pltpu.make_async_copy(
                    (own_ref, other_ref)[c].at[y, x, z, :, pl.ds(start, width)],
                    ref.at[pl.ds(row, rows), pl.ds(column, width)],
                    sems.at[first + len(copies)],
                )
            )
    return copies


def gather_whole(shard):
    whole = lax.all_gather(shard, ALL_AXES, axis=0, tiled=True)
    blocks = whole.reshape(2, Z_STEPS, 2, 2, -1, whole.shape[1])
    blocks = jnp.transpose(blocks, (3, 2, 0, 1, 4, 5))
    return blocks[0], blocks[1]


def scatter_whole(keep, send):
    blocks = jnp.transpose(jnp.stack([keep, send]), (2, 3, 1, 0, 4, 5))
    return lax.psum_scatter(
        blocks.reshape(-1, blocks.shape[-1]), ALL_AXES, scatter_dimension=0, tiled=True
    ).astype(F32)


def grad_rows_kernel(count, has_extra, edges, place_ref, a_ref, *rest):
    rest = list(rest)
    b_refs = [rest.pop(0) for _ in range(count)]
    extra_ref = rest.pop(0) if has_extra else None
    outs = [(rest.pop(0), rest.pop(0)) for _ in edges[1:]]
    held, sems = rest
    rows = outs[0][0].shape[-2]

    @pl.loop(0, a_ref.shape[1] // 256)
    def _(i):
        tile = pl.ds(pl.multiple_of(i * 256, 256), 256)
        start = 0
        for b_ref in b_refs:
            grad = dot_tn(a_ref[:, tile], b_ref[...])
            held[tile, pl.ds(start, b_ref.shape[1])] = grad.astype(BF16)
            start += b_ref.shape[1]

    if has_extra:
        held[:, pl.ds(held.shape[1] - LANES, LANES)] = extra_ref[...].astype(BF16)
    copies = []
    for pair, start, end in zip(outs, edges, edges[1:]):
        for c, y, x, z in row_blocks():
            core = lax.rem(place_ref[3] + c, 2)
            row = pl.multiple_of((block_of(place_ref, x, z, y) * 2 + core) * rows, rows)
            copies.append(
                pltpu.make_async_copy(
                    held.at[pl.ds(row, rows), pl.ds(start, end - start)],
                    pair[c].at[y, x, z],
                    sems.at[len(copies)],
                )
            )
    for copy in copies:
        copy.start()
    for copy in copies:
        copy.wait()


def grad_rows(where, a, bs, extra, edges):
    model_rows = a.shape[1]
    rows = model_rows // (2 * Z_STEPS * 2 * 2)
    width = edges[-1]
    any_spec = pl.BlockSpec(memory_space=pl.ANY)
    vmem_spec = pl.BlockSpec(memory_space=pltpu.VMEM)
    operands = (a, *bs) + (() if extra is None else (extra,))
    parts = len(edges) - 1
    outs = pl.pallas_call(
        functools.partial(grad_rows_kernel, len(bs), extra is not None, edges),
        grid_spec=pltpu.PrefetchScalarGridSpec(
            num_scalar_prefetch=1,
            grid=(1,),
            in_specs=[vmem_spec] * len(operands),
            out_specs=[any_spec] * (2 * parts),
            scratch_shapes=[
                pltpu.VMEM((model_rows, width), BF16),
                pltpu.SemaphoreType.DMA((len(row_blocks()) * parts,)),
            ],
        ),
        out_shape=[
            jax.ShapeDtypeStruct((2, 2, Z_STEPS, rows, end - start), BF16)
            for start, end in zip(edges, edges[1:])
            for _ in range(2)
        ],
        compiler_params=pltpu.CompilerParams(vmem_limit_bytes=48 * MIB),
        cost_estimate=cost(
            4 * a.shape[0] * model_rows * width, 4 * model_rows * width
        ),
        name="grad_rows",
    )(where, *operands)
    return [(outs[2 * i], outs[2 * i + 1]) for i in range(parts)]


def kept_sent(blocks, axis):
    at = 0 if axis == "y" or blocks.ndim == 4 else 1
    return [lax.index_in_dim(blocks, i, axis=at, keepdims=False) for i in range(2)]


def fold(kept, sent, axis):
    return kept.astype(F32) + swap(sent.astype(BF16), axis).astype(F32)


def rotated(values, cosine, sine):
    return values * cosine + pltpu.roll(values, HEAD_DIMENSION // 2, 1) * sine


def project_kernel(
    place_ref,
    x_ref,
    own,
    other,
    cos_ref,
    sin_ref,
    query_ref,
    kv_ref,
    normed_ref,
    weight_out,
    small_out,
    weight,
    small,
    sems,
    out_sems,
):
    step = pl.program_id(0)
    columns = weight.shape[1]
    keep = [
        pltpu.make_async_copy(weight, weight_out, out_sems.at[0]),
        pltpu.make_async_copy(small, small_out, out_sems.at[1]),
    ]

    @pl.when(step == 0)
    def _():
        copies = row_copies(
            place_ref,
            own,
            other,
            ((0, columns, weight, 0), (columns, LANES, small, 0)),
            sems,
            0,
        )
        for copy in copies:
            copy.start()
        for copy in copies:
            copy.wait()
        for copy in keep:
            copy.start()
        gain = small[...].astype(F32).T[EXPERTS : EXPERTS + 1, :]
        values = x_ref[...].astype(F32)
        normed_ref[...] = (values * rms_scale(values) * gain).astype(BF16)

    tile = KEY_VALUE_HEADS * HEAD_DIMENSION
    at = pl.ds(pl.multiple_of(step * tile, tile), tile)
    mixed = jnp.dot(normed_ref[...], weight[:, at], preferred_element_type=F32)
    query_steps = pl.num_programs(0) - 2

    def turned():
        return jnp.concatenate(
            [
                rotated(
                    mixed[:, h * HEAD_DIMENSION : (h + 1) * HEAD_DIMENSION],
                    cos_ref[...],
                    sin_ref[...],
                ).astype(BF16)
                for h in range(KEY_VALUE_HEADS)
            ],
            axis=1,
        )

    @pl.when(step < query_steps)
    def _():
        query_ref[...] = turned()

    @pl.when(step == query_steps)
    def _():
        kv_ref[...] = turned()

    @pl.when(step == query_steps + 1)
    def _():
        kv_ref[...] = mixed.astype(BF16)
        for copy in keep:
            copy.wait()


def project(where, x, pair, cosine, sine):
    rows, depth = x.shape
    columns = pair[0].shape[-1] - LANES
    tile = KEY_VALUE_HEADS * HEAD_DIMENSION
    query_steps = QUERY_HEADS // KEY_VALUE_HEADS
    whole = lambda i, *_: (0, 0)
    any_spec = pl.BlockSpec(memory_space=pl.ANY)
    turn = pl.BlockSpec((rows, HEAD_DIMENSION), whole)
    return pl.pallas_call(
        project_kernel,
        grid_spec=pltpu.PrefetchScalarGridSpec(
            num_scalar_prefetch=1,
            grid=(query_steps + 2,),
            in_specs=[pl.BlockSpec((rows, depth), whole)] + [any_spec] * 2 + [turn] * 2,
            out_specs=[
                pl.BlockSpec((rows, tile), lambda i, *_: (0, jnp.minimum(i, query_steps - 1))),
                pl.BlockSpec((rows, tile), lambda i, *_: (0, jnp.maximum(i - query_steps, 0))),
                pl.BlockSpec((rows, depth), whole),
                any_spec,
                any_spec,
            ],
            scratch_shapes=[
                pltpu.VMEM((depth, columns), BF16),
                pltpu.VMEM((depth, LANES), BF16),
                pltpu.SemaphoreType.DMA((2 * len(row_blocks()),)),
                pltpu.SemaphoreType.DMA((2,)),
            ],
        ),
        out_shape=[
            jax.ShapeDtypeStruct((rows, query_steps * tile), BF16),
            jax.ShapeDtypeStruct((rows, 2 * tile), BF16),
            jax.ShapeDtypeStruct((rows, depth), BF16),
            jax.ShapeDtypeStruct((depth, columns), BF16),
            jax.ShapeDtypeStruct((depth, LANES), BF16),
        ],
        compiler_params=pltpu.CompilerParams(vmem_limit_bytes=40 * MIB),
        cost_estimate=cost(
            6 * rows * depth * columns, 20 * MIB
        ),
        name="project",
    )(where, x, *pair, cosine, sine)


def join_kernel(
    place_ref,
    attended_ref,
    x_ref,
    gain_ref,
    own,
    other,
    middle_ref,
    normed_ref,
    scale_ref,
    weight_out,
    weight,
    sems,
    out_sems,
):
    copies = row_copies(place_ref, own, other, ((0, weight.shape[1], weight, 0),), sems, 0)
    for copy in copies:
        copy.start()
    for copy in copies:
        copy.wait()
    keep = pltpu.make_async_copy(weight, weight_out, out_sems.at[0])
    keep.start()
    wide = 512
    width = weight.shape[1]

    def join(i, total):
        at = pl.ds(pl.multiple_of(i * wide, wide), wide)
        middle = x_ref[:, at].astype(F32) + jnp.dot(
            attended_ref[...], weight[:, at], preferred_element_type=F32
        )
        middle_ref[:, at] = middle
        return total + jnp.sum(middle * middle, axis=1, keepdims=True)

    total = lax.fori_loop(0, width // wide, join, jnp.zeros((x_ref.shape[0], 1), F32))
    scale = lax.rsqrt(total / width + NORM_EPS)
    scale_ref[...] = scale
    normed_ref[...] = (middle_ref[...] * scale * gain_ref[...]).astype(BF16)
    keep.wait()


def join(where, attended, x, gain, pair):
    rows, depth = attended.shape
    width = pair[0].shape[-1]
    any_spec = pl.BlockSpec(memory_space=pl.ANY)
    vmem_spec = pl.BlockSpec(memory_space=pltpu.VMEM)
    return pl.pallas_call(
        join_kernel,
        grid_spec=pltpu.PrefetchScalarGridSpec(
            num_scalar_prefetch=1,
            grid=(1,),
            in_specs=[vmem_spec] * 3 + [any_spec] * 2,
            out_specs=[vmem_spec] * 3 + [any_spec],
            scratch_shapes=[
                pltpu.VMEM((depth, width), BF16),
                pltpu.SemaphoreType.DMA((len(row_blocks()),)),
                pltpu.SemaphoreType.DMA((1,)),
            ],
        ),
        out_shape=[
            jax.ShapeDtypeStruct((rows, width), F32),
            jax.ShapeDtypeStruct((rows, width), BF16),
            jax.ShapeDtypeStruct((rows, 1), F32),
            jax.ShapeDtypeStruct((depth, width), BF16),
        ],
        compiler_params=pltpu.CompilerParams(vmem_limit_bytes=40 * MIB),
        cost_estimate=cost(
            4 * rows * depth * width, 16 * MIB
        ),
        name="join",
    )(where, attended, x, gain, *pair)


def score_pair(q, ko_ref, kp_ref, seg_col, seg_own, seg_prev):
    scale = HEAD_DIMENSION ** (-0.5)
    own = dot_nt(q, ko_ref[...]) * scale
    query_at = lax.broadcasted_iota(jnp.int32, own.shape, 0)
    key_at = lax.broadcasted_iota(jnp.int32, own.shape, 1)
    own = jnp.where((seg_col == seg_own) & (key_at <= query_at), own, MASKED_SCORE)
    if kp_ref is None:
        return (own,)
    prev = dot_nt(q, kp_ref[...]) * scale
    return (own, jnp.where(seg_col == seg_prev, prev, MASKED_SCORE))


def attend_kernel(
    half_ref, q_ref, ko_ref, vo_ref, kp_ref, vp_ref, sc_ref, so_ref, sp_ref, out_ref, log_ref
):
    def run(with_previous):
        parts = score_pair(
            q_ref[...],
            ko_ref,
            kp_ref if with_previous else None,
            sc_ref[...],
            so_ref[...],
            sp_ref[...],
        )
        highest = jnp.max(parts[0], axis=-1, keepdims=True)
        for part in parts[1:]:
            highest = jnp.maximum(highest, jnp.max(part, axis=-1, keepdims=True))
        exponents = [jnp.exp(part - highest) for part in parts]
        total = sum(jnp.sum(part, axis=-1, keepdims=True) for part in exponents)
        scale = 1.0 / total
        mixed = sum(
            jnp.dot((part * scale).astype(BF16), ref[...], preferred_element_type=F32)
            for part, ref in zip(exponents, (vo_ref, vp_ref))
        )
        out_ref[...] = mixed.astype(BF16)
        log_ref[0] = highest + jnp.log(total)

    pl.when(half_ref[0] == 0)(lambda: run(False))
    pl.when(half_ref[0] != 0)(lambda: run(True))


def head_specs(rows):
    group = QUERY_HEADS // KEY_VALUE_HEADS
    query = pl.BlockSpec((rows, HEAD_DIMENSION), lambda h, *_: (0, h))
    key = pl.BlockSpec((rows, HEAD_DIMENSION), lambda h, *_: (0, h // group))
    value = pl.BlockSpec((rows, HEAD_DIMENSION), lambda h, *_: (0, KEY_VALUE_HEADS + h // group))
    col = pl.BlockSpec((rows, 1), lambda h, *_: (0, 0))
    row = pl.BlockSpec((1, rows), lambda h, *_: (0, 0))
    log = pl.BlockSpec((1, rows, 1), lambda h, *_: (h, 0, 0))
    return query, [query, key, value, key, value, col, row, row], log


def attend(queries, own, previous, seg_col, seg_own, seg_prev, half):
    rows = queries.shape[0]
    query, specs, log = head_specs(rows)
    return pl.pallas_call(
        attend_kernel,
        grid_spec=pltpu.PrefetchScalarGridSpec(
            num_scalar_prefetch=1,
            grid=(QUERY_HEADS,),
            in_specs=specs,
            out_specs=[query, log],
        ),
        out_shape=[
            jax.ShapeDtypeStruct((rows, QUERY_HEADS * HEAD_DIMENSION), BF16),
            jax.ShapeDtypeStruct((QUERY_HEADS, rows, 1), F32),
        ],
        compiler_params=pltpu.CompilerParams(vmem_limit_bytes=40 * MIB),
        cost_estimate=cost(
            8 * rows * rows * QUERY_HEADS * HEAD_DIMENSION, 16 * MIB, 2 * rows * rows * QUERY_HEADS
        ),
        name="attend",
    )(half, queries, own, own, previous, previous, seg_col, seg_own, seg_prev)


def attend_back_kernel(
    half_ref,
    q_ref,
    ko_ref,
    vo_ref,
    kp_ref,
    vp_ref,
    sc_ref,
    so_ref,
    sp_ref,
    up_ref,
    log_ref,
    cos_ref,
    sin_ref,
    dq_ref,
    dko_ref,
    dvo_ref,
    dkp_ref,
    dvp_ref,
):
    scale = HEAD_DIMENSION ** (-0.5)
    first = lax.rem(pl.program_id(0), QUERY_HEADS // KEY_VALUE_HEADS) == 0

    @pl.when(first)
    def _():
        for ref in (dko_ref, dvo_ref, dkp_ref, dvp_ref):
            ref[...] = jnp.zeros_like(ref)

    def run(with_previous):
        q, up = q_ref[...], up_ref[...]
        parts = score_pair(
            q, ko_ref, kp_ref if with_previous else None, sc_ref[...], so_ref[...], sp_ref[...]
        )
        weights = [jnp.exp(part - log_ref[0]) for part in parts]
        grads = [dot_nt(up, ref[...]) for ref, _ in zip((vo_ref, vp_ref), parts)]
        inner = sum(
            jnp.sum(w * g, axis=-1, keepdims=True) for w, g in zip(weights, grads)
        )
        scores = [(w * (g - inner)).astype(BF16) for w, g in zip(weights, grads)]
        dq = sum(
            jnp.dot(s, ref[...], preferred_element_type=F32)
            for s, ref in zip(scores, (ko_ref, kp_ref))
        )
        dq = (dq * scale).astype(BF16).astype(F32)
        dq_ref[...] = rotated(dq, cos_ref[...], sin_ref[...]).astype(BF16)
        for s, w, dk_ref, dv_ref in zip(scores, weights, (dko_ref, dkp_ref), (dvo_ref, dvp_ref)):
            dk_ref[...] += dot_tn(s, q) * scale
            dv_ref[...] += dot_tn(w.astype(BF16), up)

    pl.when(half_ref[0] == 0)(lambda: run(False))
    pl.when(half_ref[0] != 0)(lambda: run(True))


def attend_back(queries, own, previous, seg_col, seg_own, seg_prev, half, up, log_sums, cosine, sine):
    rows = queries.shape[0]
    query, specs, log = head_specs(rows)
    group = QUERY_HEADS // KEY_VALUE_HEADS
    turn = pl.BlockSpec((rows, HEAD_DIMENSION), lambda h, *_: (0, 0))
    kv = pl.BlockSpec((rows, HEAD_DIMENSION), lambda h, *_: (0, h // group))
    kv_shape = jax.ShapeDtypeStruct((rows, KEY_VALUE_HEADS * HEAD_DIMENSION), F32)
    return pl.pallas_call(
        attend_back_kernel,
        grid_spec=pltpu.PrefetchScalarGridSpec(
            num_scalar_prefetch=1,
            grid=(QUERY_HEADS,),
            in_specs=specs + [query, log, turn, turn],
            out_specs=[query, kv, kv, kv, kv],
        ),
        out_shape=[jax.ShapeDtypeStruct((rows, QUERY_HEADS * HEAD_DIMENSION), BF16)]
        + [kv_shape] * 4,
        compiler_params=pltpu.CompilerParams(vmem_limit_bytes=48 * MIB),
        cost_estimate=cost(
            20 * rows * rows * QUERY_HEADS * HEAD_DIMENSION, 24 * MIB, 2 * rows * rows * QUERY_HEADS
        ),
        name="attend_back",
    )(
        half,
        queries,
        own,
        own,
        previous,
        previous,
        seg_col,
        seg_own,
        seg_prev,
        up,
        log_sums,
        cosine,
        sine,
    )


def expert_kernel(count, given, gives, grads_too, place_ref, *refs):
    refs = list(refs)
    pop = lambda n: [refs.pop(0) for _ in range(n)]
    pieces = pop(4)
    x_refs, t_refs = pop(count), pop(count)
    rank_row_ref, rank_col_ref, router_ref = pop(3)
    given_refs = pop(4) if given else []
    mix_refs, ffn_refs = pop(count), pop(count)
    (gate_grad_ref,) = pop(1)
    gives_refs = pop(4) if gives else []
    grads = pop(4) if grads_too else []
    (
        in_w,
        down_w,
        picked,
        joined_grad,
        active,
        slot_grad,
        top,
        spread,
        gates,
        x_held,
        t_held,
        sems,
        token_sems,
        given_sems,
    ) = refs
    in_rows = in_w.shape[0] // (4 * Z_STEPS)
    down_rows = down_w.shape[0] // (4 * Z_STEPS)
    tokens, width = x_refs[0].shape
    hidden = active.shape[1]
    slots = count * CAP
    own_slots = pl.ds(0, slots)
    wide, narrow = 512, 256

    def block_copies(outward, which):
        copies = []
        for (y, x), piece in zip(
            itertools.product(range(2), range(2)), grads if outward else pieces
        ):
            for z in range(Z_STEPS):
                block = (lax.rem(place_ref[0] + x, 2) * Z_STEPS + z) * 2 + lax.rem(
                    place_ref[2] + y, 2
                )
                whole, rows, start = (
                    (in_w, in_rows, 0) if which == 0 else (down_w, down_rows, in_rows)
                )
                ends = (
                    piece.at[z, pl.ds(start, rows), :],
                    whole.at[pl.ds(pl.multiple_of(block * rows, rows), rows), :],
                )
                if outward:
                    ends = ends[::-1]
                copies.append(pltpu.make_async_copy(*ends, sems.at[which, len(copies)]))
        return copies

    def token_copies(s):
        return [
            pltpu.make_async_copy(many[s], held.at[s % 2], token_sems.at[i, s % 2])
            for i, (many, held) in enumerate(((x_refs, x_held), (t_refs, t_held)))
        ]

    kept = (picked, joined_grad, active, slot_grad)
    arriving = [
        pltpu.make_async_copy(
            ref, held.at[pl.ds(slots, held.shape[0] - slots), :], given_sems.at[i]
        )
        for i, (ref, held) in enumerate(zip(given_refs, kept))
    ]
    leaving = [
        pltpu.make_async_copy(held.at[own_slots, :], ref, given_sems.at[i])
        for i, (ref, held) in enumerate(zip(gives_refs, kept))
    ]
    weight_copies = block_copies(False, 0) + block_copies(False, 1)
    for copy in token_copies(0) + weight_copies + arriving:
        copy.start()

    for s in range(count):
        for copy in token_copies(s):
            copy.wait()
        if s + 1 < count:
            for copy in token_copies(s + 1):
                copy.start()
        at_slots = slice(s * CAP, (s + 1) * CAP)
        chosen = (
            lax.broadcasted_iota(jnp.int32, (CAP, tokens), 0) == rank_row_ref[s]
        ).astype(F32)
        spread[s] = (
            (lax.broadcasted_iota(jnp.int32, (tokens, CAP), 1) == rank_col_ref[s])
            .astype(F32)
            .astype(BF16)
        )
        expert_row = lax.broadcasted_iota(jnp.int32, (router_ref.shape[0], tokens), 0)
        logits = jnp.where(
            expert_row < EXPERTS, dot_nt(router_ref[...], x_held[s % 2]), MASKED_SCORE
        )
        exponent = jnp.exp(logits - jnp.max(logits, axis=0, keepdims=True))
        probs = exponent / jnp.sum(exponent, axis=0, keepdims=True)
        gate_row = jnp.sum(
            jnp.where(expert_row == place_ref[4], probs, 0.0), axis=0, keepdims=True
        )
        gate = jnp.sum(chosen * gate_row, axis=1, keepdims=True)
        gates[at_slots, :] = gate
        pick = chosen.astype(BF16)

        @pl.loop(0, width // wide)
        def _(i, s=s, pick=pick, gate=gate, at_slots=at_slots):
            at = pl.ds(pl.multiple_of(i * wide, wide), wide)
            picked[at_slots, at] = jnp.dot(
                pick, x_held[s % 2, :, at], preferred_element_type=F32
            ).astype(BF16)
            top_rows = jnp.dot(pick, t_held[s % 2, :, at], preferred_element_type=F32)
            top[at_slots, at] = top_rows.astype(BF16)
            slot_grad[at_slots, at] = (gate * top_rows).astype(BF16)

    for copy in weight_copies:
        copy.wait()

    @pl.loop(0, hidden // narrow)
    def _(i):
        at = pl.ds(pl.multiple_of(i * narrow, narrow), narrow)
        up_at = pl.ds(pl.multiple_of(hidden + i * narrow, narrow), narrow)
        rows = picked[own_slots, :]
        gate_part = jnp.dot(rows, in_w[:, at], preferred_element_type=F32)
        up_part = jnp.dot(rows, in_w[:, up_at], preferred_element_type=F32)
        act_grad = dot_nt(slot_grad[own_slots, :], down_w[at, :])
        sigmoid = jax.nn.sigmoid(gate_part)
        silu = gate_part * sigmoid
        active[own_slots, at] = (silu * up_part).astype(BF16)
        joined_grad[own_slots, at] = (
            act_grad * up_part * sigmoid * (1.0 + gate_part * (1.0 - sigmoid))
        ).astype(BF16)
        joined_grad[own_slots, up_at] = (act_grad * silu).astype(BF16)

    for copy in leaving:
        copy.start()

    def results(i, total):
        at = pl.ds(pl.multiple_of(i * wide, wide), wide)
        result = jnp.dot(active[own_slots, :], down_w[:, at], preferred_element_type=F32)
        mix = (gates[...] * result).astype(BF16)
        back = dot_nt(joined_grad[own_slots, :], in_w[at, :]).astype(BF16)
        for s in range(count):
            at_slots = slice(s * CAP, (s + 1) * CAP)
            for rows, out in ((mix, mix_refs[s]), (back, ffn_refs[s])):
                out[:, at] = jnp.dot(
                    spread[s], rows[at_slots], preferred_element_type=F32
                ).astype(BF16)
        return total + jnp.sum(result * top[:, at].astype(F32), axis=1, keepdims=True)

    gate_grad = lax.fori_loop(0, width // wide, results, jnp.zeros((slots, 1), F32))
    for s in range(count):
        chosen = lax.broadcasted_iota(jnp.int32, (CAP, tokens), 0) == rank_row_ref[s]
        gate_grad_ref[s] = jnp.sum(
            jnp.where(chosen, gate_grad[s * CAP : (s + 1) * CAP], 0.0), axis=0, keepdims=True
        )
    for copy in arriving + leaving:
        copy.wait()

    if grads_too:
        down_w[...] = dot_tn(active[...], slot_grad[...]).astype(BF16)

        down_copies = block_copies(True, 1)
        for copy in down_copies:
            copy.start()

        @pl.loop(0, width // hidden)
        def _(i):
            at = pl.ds(pl.multiple_of(i * hidden, hidden), hidden)
            in_w[at, :] = dot_tn(picked[:, at], joined_grad[...]).astype(BF16)

        in_copies = block_copies(True, 0)
        for copy in in_copies:
            copy.start()
        for copy in down_copies + in_copies:
            copy.wait()


def expert_pass(where, pieces, x_some, t_some, rank, router_rows, given, gives, grads_too):
    count = len(x_some)
    tokens, width = x_some[0].shape
    hidden = F
    slots = count * CAP
    held_slots = slots + (given[0].shape[0] if given else 0)
    any_spec = pl.BlockSpec(memory_space=pl.ANY)
    vmem_spec = pl.BlockSpec(memory_space=pltpu.VMEM)
    token_shape = jax.ShapeDtypeStruct((tokens, width), BF16)
    kept_widths = (width, 2 * hidden, hidden, width)
    flops = 2 * slots * width * hidden * 9 + 8 * slots * tokens * width
    outs = pl.pallas_call(
        functools.partial(expert_kernel, count, bool(given), gives, grads_too),
        grid_spec=pltpu.PrefetchScalarGridSpec(
            num_scalar_prefetch=1,
            grid=(1,),
            in_specs=[any_spec] * (len(pieces) + 2 * count)
            + [vmem_spec] * 3
            + [any_spec] * len(given),
            out_specs=[vmem_spec] * (2 * count + 1)
            + [any_spec] * (4 * gives + 4 * grads_too),
            scratch_shapes=[
                pltpu.VMEM((width, 2 * hidden), BF16),
                pltpu.VMEM((hidden, width), BF16),
                pltpu.VMEM((held_slots, width), BF16),
                pltpu.VMEM((held_slots, 2 * hidden), BF16),
                pltpu.VMEM((held_slots, hidden), BF16),
                pltpu.VMEM((held_slots, width), BF16),
                pltpu.VMEM((slots, width), BF16),
                pltpu.VMEM((count, tokens, CAP), BF16),
                pltpu.VMEM((slots, 1), F32),
                pltpu.VMEM((2, tokens, width), BF16),
                pltpu.VMEM((2, tokens, width), BF16),
                pltpu.SemaphoreType.DMA((2, 4 * Z_STEPS)),
                pltpu.SemaphoreType.DMA((2, 2)),
                pltpu.SemaphoreType.DMA((4,)),
            ],
        ),
        out_shape=[token_shape] * (2 * count)
        + [jax.ShapeDtypeStruct((count, 1, tokens), F32)]
        + [jax.ShapeDtypeStruct((slots, w), BF16) for w in kept_widths if gives]
        + [jax.ShapeDtypeStruct(p.shape, BF16) for p in pieces if grads_too],
        compiler_params=pltpu.CompilerParams(vmem_limit_bytes=60 * MIB),
        cost_estimate=cost(
            8 * flops, 96 * MIB, slots * hidden
        ),
        name="expert",
    )(where, *pieces, *x_some, *t_some, *rank, router_rows, *given)
    rest = list(outs[2 * count + 1 :])
    kept = [rest.pop(0) for _ in range(4 * gives)]
    return outs[:count], outs[count : 2 * count], outs[2 * count], kept, rest


def expert_pairs(expert_in, expert_down):
    core = lax.axis_index("core")
    low = jnp.concatenate([expert_in.astype(BF16), expert_down.astype(BF16)], axis=1)
    low = low.reshape(2, 2, OWN_EXPERTS, *low.shape[1:])
    return by_index(core, take_index(core, low, 1), swap(take_index(1 - core, low, 1), "core"))


def expert_halves(pair, number, in_rows):
    x = lax.axis_index("x")
    pair = pair[:, :, number]
    width = pair.shape[-1]
    both = jnp.concatenate(
        [
            jnp.swapaxes(part, 0, 1).reshape(2, -1, width)
            for part in (pair[:, :, :in_rows], pair[:, :, in_rows:])
        ],
        axis=1,
    )
    return take_index(x, both, 0), take_index(1 - x, both, 0)


def gather_expert_whole(pair, number, in_rows):
    own, sent = expert_halves(pair, number, in_rows)
    chunk = by_index(lax.axis_index("x"), own, swap(sent, "x"))
    whole = lax.all_gather(chunk, ("z", "y"))
    rows = chunk.shape[1] * 2 // 3
    width = chunk.shape[2]
    parts = [
        jnp.moveaxis(part, 0, 1).reshape(2, Z_STEPS, 2, -1, width)
        for part in (whole[:, :, :rows], whole[:, :, rows:])
    ]
    both = jnp.concatenate(parts, axis=3)
    return [both[x, :, y] for y in range(2) for x in range(2)]


def scatter_expert_whole(grads):
    spots = lax.axis_size("z") * 2
    both = jnp.stack(grads).reshape((2, 2) + grads[0].shape)
    both = jnp.transpose(both, (1, 2, 0, 3, 4))
    width = both.shape[-1]
    in_rows = both.shape[3] * 2 // 3
    parts = [
        part.reshape(2, spots, -1, width)
        for part in (both[:, :, :, :in_rows], both[:, :, :, in_rows:])
    ]
    both = jnp.moveaxis(jnp.concatenate(parts, axis=2), 1, 0)
    total = lax.psum_scatter(both, ("z", "y"), scatter_dimension=0)
    x = lax.axis_index("x")
    return take_index(x, total, 0), take_index(1 - x, total, 0)


def finish_expert(sums, in_rows):
    x, core = lax.axis_index("x"), lax.axis_index("core")
    width = sums[0].shape[-1]
    both = by_index(x, sums[0], swap(sums[1], "x"))
    split = jnp.concatenate(
        [
            both[:, : 2 * in_rows].reshape(2, 2, in_rows, width),
            both[:, 2 * in_rows :].reshape(2, 2, -1, width),
        ],
        axis=2,
    )
    other = swap(take_index(1 - core, split, 1), "core")
    both = jnp.swapaxes(by_index(core, take_index(core, split, 1), other), 0, 1).astype(F32)
    return both[:, :, :in_rows], both[:, :, in_rows:]


def shards(
    tokens,
    cotangent,
    segment_ids,
    route_ids,
    query_key_value_weight,
    out_weight,
    router_weight,
    expert_in,
    expert_down,
    norm_gains,
    query_key_value_moment,
    out_moment,
    router_moment,
    in_moment,
    down_moment,
    gains_moment,
    query_key_value_second,
    out_second,
    router_second,
    in_second,
    down_second,
    gains_second,
):
    local_rows = tokens.shape[1]
    model_width = tokens.shape[2]
    staged = lax.axis_size("z") == Z_STEPS
    x_index = lax.axis_index("x")
    shard_rows = query_key_value_weight.shape[0]
    in_rows, down_rows = expert_in.shape[1], expert_down.shape[1]
    key_width = KEY_VALUE_HEADS * HEAD_DIMENSION
    first_expert = (x_index * 2 + lax.axis_index("core")) * OWN_EXPERTS
    where = place() if staged else jnp.zeros((4,), jnp.int32)
    x_tokens, top = tokens[0], cotangent[0]

    own_gains = norm_gains.astype(BF16)
    small_part = jnp.concatenate(
        [
            router_weight.astype(BF16),
            own_gains,
            jnp.zeros((shard_rows, LANES - EXPERTS - 2), BF16),
        ],
        axis=1,
    )
    qkv_own = query_key_value_weight.astype(BF16)
    qkv_width = qkv_own.shape[1]
    half_width = qkv_width // 2
    attention_own = jnp.concatenate([qkv_own, small_part, out_weight.astype(BF16)], axis=1)
    attention_edges = (0, half_width, qkv_width + LANES, attention_own.shape[1])

    segments = segment_ids[0]
    named = jnp.concatenate([route_ids[0].T, segments[None]])
    named_x = swap(named, "x")
    named_core = swap(jnp.stack([named, named_x]), "core")
    routes_all = jnp.stack([part[:TOPK] for part in (named, named_x, *named_core)])
    seg_prev = named_x[TOPK]
    (top_sent,) = hold((top,), named_x) if staged else (top,)
    top_x = swap(top_sent, "x")

    pair = expert_pairs(expert_in, expert_down)
    gather_z = lambda half: lax.all_gather(half, "z")
    if staged:
        attention_z = [rotate(attention_own, -k) for k in range(1, Z_STEPS)]
        own_one, sent_one = expert_halves(pair, 0, in_rows)
        first_held, second_held, out_held = (
            jnp.stack([part[:, start:end] for part in (attention_own, *attention_z)])
            for start, end in zip(attention_edges, attention_edges[1:])
        )
        first_held, second_held, own_one, seg_prev, routes_all = hold(
            (first_held, second_held, own_one, seg_prev, routes_all), sent_one
        )
        one_own = gather_z(own_one)
        first_x = swap(first_held, "x")
        second_y = swap(second_held, "y")
        other_one = swap(sent_one, "x")
        first_held = jnp.stack([first_held, first_x])
        second_held = jnp.stack([second_held, second_y])
        first_held, other_one, top_x = hold((first_held, other_one, top_x))
        first_y = swap(first_held, "y")
        second_x = swap(second_held, "x")
        one_other = gather_z(other_one)
        first_held = jnp.stack([first_held, first_y])
        second_held = jnp.stack([second_held, second_x], axis=1)
        qkv_held = jnp.concatenate([first_held, second_held], axis=-1)
        (out_held,) = hold((out_held,), first_y, second_x)
        qkv_held, one_own = hold((qkv_held, one_own))
        out_x = swap(out_held, "x")
        qkv_core = swap(qkv_held, "core")
        one_own_y = swap(one_own, "y")
        qkv_pair = (qkv_held, qkv_core)
    else:
        qkv_pair, out_pair = (
            gather_whole(part)
            for part in (
                attention_own[:, : qkv_width + LANES],
                attention_own[:, qkv_width + LANES :],
            )
        )
        pieces_one, pieces_two = (gather_expert_whole(pair, i, in_rows) for i in range(2))

    half_size = HEAD_DIMENSION // 2
    positions = (x_index * local_rows + jnp.arange(local_rows, dtype=jnp.int32)).astype(F32)
    frequency = ROPE_BASE ** (-2.0 * jnp.arange(half_size, dtype=F32) / HEAD_DIMENSION)
    angles = positions[:, None] * frequency[None, :]
    cosine, sine = jnp.cos(angles), jnp.sin(angles)
    cosine = jnp.concatenate([cosine, cosine], axis=1)
    sine_forward = jnp.concatenate([-sine, sine], axis=1)
    half = x_index.astype(jnp.int32).reshape(1)

    experts_here = first_expert + jnp.arange(OWN_EXPERTS, dtype=jnp.int32)
    member = jnp.any(routes_all[None] == experts_here[:, None, None, None], axis=2)
    earlier = (
        lax.broadcasted_iota(jnp.int32, (local_rows, local_rows), 0)
        < lax.broadcasted_iota(jnp.int32, (local_rows, local_rows), 1)
    ).astype(BF16)
    rank = jnp.dot(
        member.astype(BF16).reshape(-1, local_rows), earlier, preferred_element_type=F32
    ).reshape(member.shape)
    rank = jnp.where(member, rank.astype(jnp.int32), -1)

    queries, kv_own, normed, qkv_low, small_low = project(
        where, x_tokens, qkv_pair, cosine, sine_forward
    )
    kv_prev = swap(kv_own, "x")
    attn_gain = small_low[:, EXPERTS].astype(F32)
    ffn_gain = small_low[:, EXPERTS + 1].astype(F32)
    router_rows = small_low.T[:16]
    if staged:
        own_two, sent_two = expert_halves(pair, 1, in_rows)
        kv_prev, out_x, one_own_y, one_other, own_two, sent_two = hold(
            (kv_prev, out_x, one_own_y, one_other, own_two, sent_two)
        )
        out_held = jnp.stack([out_held, out_x])
        out_y = swap(out_held, "y")
        other_two = swap(sent_two, "x")
        two_own = gather_z(own_two)
    segs = (segments[:, None], segments[None, :], seg_prev[None, :])
    attended, log_sums = attend(queries, kv_own, kv_prev, *segs, half)
    top_core, top_both = swap(top, "core"), swap(top_x, "core")
    if staged:
        attended, out_y, other_two = hold((attended, out_y, other_two))
        out_held = jnp.stack([out_held, out_y])
        out_pair = (out_held, swap(out_held, "core"))
        one_other_y = swap(one_other, "y")
        two_other = gather_z(other_two)
    middle, normed_ffn, second_scale, out_low = join(
        where, attended, x_tokens, ffn_gain[None, :], out_pair
    )

    ffn_core = swap(normed_ffn, "core")
    ffn_x = swap(normed_ffn, "x")
    if staged:
        ffn_x, two_own = hold((ffn_x, two_own))
        two_own_y = swap(two_own, "y")
    ffn_both = swap(ffn_x, "core")
    x_all = (normed_ffn, ffn_x, ffn_core, ffn_both)
    t_all = (top, top_x, top_core, top_both)
    places = [jnp.concatenate([where, first_expert[None] + i]) for i in range(OWN_EXPERTS)]
    if staged:
        two_other, ffn_both = hold((two_other, ffn_both))
        x_all = (normed_ffn, ffn_x, ffn_core, ffn_both)
        pieces_one = (one_own, one_other, one_own_y, one_other_y)
        pieces_two = (two_own, two_other, two_own_y, swap(two_other, "y"))

    def expert(i, pieces, sources, given, gives, grads_too):
        some = lambda parts: [parts[s] for s in sources]
        ranks = (
            jnp.stack(some(rank[i]))[:, None, :],
            jnp.stack(some(rank[i]))[:, :, None],
        )
        return expert_pass(
            places[i], pieces, some(x_all), some(t_all), ranks, router_rows, given, gives, grads_too
        )

    mix_one, ffn_one, gates_one, _, grads_one = expert(
        0, pieces_one, (0, 1, 2, 3), (), False, True
    )
    if staged:
        back_one = [swap(part, "y") for part in grads_one[2:]]
        pieces_two = hold(pieces_two, gates_one)
    mix_far, ffn_far, gates_far, kept_far, _ = expert(1, pieces_two, (1, 3), (), True, False)
    add = lambda *parts: sum(part.astype(F32) for part in parts)
    ffn_come = swap(add(ffn_one[3], ffn_far[1]).astype(BF16), "core")
    ffn_crossed = swap(add(ffn_one[1], ffn_far[0], ffn_come).astype(BF16), "x")
    if staged:
        total_one = [add(grads_one[0], back_one[0]).astype(BF16)]
        kept_far[0], total_one[0] = hold((kept_far[0], total_one[0]), ffn_come)
        sums_one = [lax.psum_scatter(total_one[0], "z", scatter_dimension=0)]
    mix_near, ffn_near, gates_near, _, grads_two = expert(
        1, pieces_two, (0, 2), tuple(kept_far), False, True
    )
    gates_two = jnp.stack([gates_near[0], gates_far[0], gates_near[1], gates_far[1]])

    if staged:
        back_two = [swap(part, "y") for part in grads_two[2:]]
        total_one.append(add(grads_one[1], back_one[1]).astype(BF16))
        sums_one.append(lax.psum_scatter(total_one[1], "z", scatter_dimension=0))
    else:
        sums_one, sums_two = (scatter_expert_whole(grads) for grads in (grads_one, grads_two))
    ffn_back, ffn_crossed = hold((ffn_near[1], ffn_crossed))
    ffn_arrived = swap(add(ffn_one[2], ffn_back).astype(BF16), "core")
    gate_grad = jnp.concatenate([gates_one, gates_two], axis=1)
    spread = lax.dynamic_update_slice_in_dim(
        jnp.zeros((SOURCES, EXPERTS, local_rows), F32), gate_grad, first_expert, axis=1
    )
    spread_core = swap(spread[2:], "core")
    spread_x = swap(spread[1] + spread_core[1], "x")
    prob_grad = (spread[0] + spread_core[0] + spread_x).T
    if staged:
        ffn_crossed, sums_one[0] = hold((ffn_crossed, sums_one[0]), total_one[1])
    ffn_grad = add(ffn_one[0], ffn_near[0], ffn_arrived, ffn_crossed)
    (mix_sent,) = hold((mix_far[1],), ffn_crossed)
    mix_come = swap(add(mix_one[3], mix_sent).astype(BF16), "core")
    mix_arrived = swap(add(mix_one[2], mix_near[1]).astype(BF16), "core")
    mix_crossed = swap(add(mix_one[1], mix_far[0], mix_come).astype(BF16), "x")

    logits = jnp.dot(normed_ffn, small_low[:, :EXPERTS], preferred_element_type=F32)
    exponent = jnp.exp(logits - jnp.max(logits, axis=-1, keepdims=True))
    router_probs = exponent / jnp.sum(exponent, axis=-1, keepdims=True)
    logit_grad = router_probs * (
        prob_grad - jnp.sum(router_probs * prob_grad, axis=-1, keepdims=True)
    )
    router_grad = jnp.dot(normed_ffn.astype(F32).T, logit_grad, precision=PRECISE)
    ffn_grad = ffn_grad + jnp.dot(
        logit_grad, small_low[:, :EXPERTS].astype(F32).T, precision=PRECISE
    )
    ffn_gain_grad = jnp.sum(middle * second_scale * ffn_grad, axis=0)
    middle_grad = top.astype(F32) + norm_value_grad(middle, second_scale, ffn_gain, ffn_grad)
    branch_grad = middle_grad.astype(BF16)
    attended_grad = dot_nt(branch_grad, out_low).astype(BF16)
    small_grad = jnp.concatenate(
        [
            router_grad,
            ffn_gain_grad[:, None],
            jnp.zeros((model_width, LANES - EXPERTS - 1), F32),
        ],
        axis=1,
    )
    (out_blocks,) = grad_rows(
        where.at[1].set(0),
        attended, (branch_grad,),
        small_grad,
        (0, model_width + LANES),
    )
    if staged:
        attended_grad, back_two[0] = hold((attended_grad, back_two[0]), out_blocks[1])
        total_two = [add(grads_two[0], back_two[0]).astype(BF16)]
        sums_two = [lax.psum_scatter(total_two[0], "z", scatter_dimension=0)]
        out_kept, out_sent = kept_sent(fold(*out_blocks, "core"), "y")
        out_come = swap(out_sent.astype(BF16), "y")
    query_grad, key_own, value_own, key_prev, value_prev = attend_back(
        queries, kv_own, kv_prev, *segs, half, attended_grad, log_sums, cosine, -sine_forward
    )
    crossed = swap(jnp.concatenate([key_prev, value_prev], axis=1).astype(BF16), "x")
    if staged:
        crossed, back_two[1], mix_crossed = hold(
            (crossed, back_two[1], mix_crossed), query_grad
        )
        total_two.append(add(grads_two[1], back_two[1]).astype(BF16))
        sums_two.append(lax.psum_scatter(total_two[1], "z", scatter_dimension=0))
    crossed = crossed.astype(F32)
    key_grad = (key_own + crossed[:, :key_width]).astype(BF16).astype(F32)
    value_grad = value_own + crossed[:, key_width:]
    key_grad = key_grad.reshape(local_rows, KEY_VALUE_HEADS, HEAD_DIMENSION)
    key_grad = key_grad * cosine[:, None, :] - jnp.roll(key_grad, half_size, axis=2) * sine_forward[
        :, None, :
    ]
    kv_grad = jnp.concatenate(
        [key_grad.reshape(local_rows, key_width).astype(BF16), value_grad.astype(BF16)], axis=1
    )
    if staged:
        kv_grad, out_come, sums_one[1] = hold((kv_grad, out_come, sums_one[1]))
        out_kept, out_sent = kept_sent(out_kept + out_come.astype(F32), "x")
        out_come = swap(out_sent.astype(BF16), "x")
    qkv_blocks = grad_rows(
        where.at[1].set(0), normed, (query_grad, kv_grad), None, (0, half_width, 2 * half_width)
    )
    if staged:
        (out_come,) = hold((out_come,), qkv_blocks[0][1])
        first = fold(*qkv_blocks[0], "core")
        second = fold(*qkv_blocks[1], "core")
        first_kept, first_sent = kept_sent(first, "y")
        second_kept, second_sent = kept_sent(second, "x")
        first_come = swap(first_sent.astype(BF16), "y")
        second_come = swap(second_sent.astype(BF16), "x")
        first_kept, first_sent = kept_sent(first_kept + first_come.astype(F32), "x")
        second_kept, second_sent = kept_sent(second_kept + second_come.astype(F32), "y")
        *sums_one, sums_two[0], out_come = hold(
            (*sums_one, sums_two[0], out_come), first_come, second_come, total_two[1]
        )
        out_total = (out_kept + out_come.astype(F32)).astype(BF16)
        first_come = swap(first_sent.astype(BF16), "x")
        second_come = swap(second_sent.astype(BF16), "y")
        expert_sums = [finish_expert(sums_one, in_rows)]
        sums_two = hold(sums_two, first_come, second_come)
        expert_sums.append(finish_expert(sums_two, in_rows))
        first = first_kept + first_come.astype(F32)
        second = second_kept + second_come.astype(F32)
        rows_total = jnp.concatenate([first.astype(BF16), second.astype(BF16), out_total], axis=-1)
        rows_sum = lax.psum_scatter(rows_total, "z", scatter_dimension=0).astype(F32)
        qkv_sum, out_rows = rows_sum[:, :qkv_width], rows_sum[:, qkv_width:]
    else:
        expert_sums = [finish_expert(sums, in_rows) for sums in (sums_one, sums_two)]
        out_rows = scatter_whole(*out_blocks)
        qkv_sum = jnp.concatenate([scatter_whole(*blocks) for blocks in qkv_blocks], axis=1)
    in_sum, down_sum = (jnp.stack(parts, axis=2) for parts in zip(*expert_sums))
    in_sum = in_sum.reshape(expert_in.shape)
    down_sum = down_sum.reshape(expert_down.shape)
    mixture = add(mix_one[0], mix_near[0], mix_arrived, mix_crossed)
    output = (middle + mixture).astype(BF16)
    mixed_grad = jnp.concatenate([query_grad, kv_grad], axis=1)
    inputs = x_tokens.astype(F32)
    input_grad = middle_grad + norm_value_grad(
        inputs, rms_scale(inputs), attn_gain, dot_nt(mixed_grad, qkv_low)
    )

    out_sum = out_rows[:, :model_width]
    router_sum = out_rows[:, model_width : model_width + EXPERTS]
    attn_gain_sum = jnp.sum(qkv_sum * qkv_own.astype(F32), axis=1) / own_gains[:, 0].astype(F32)
    gains_sum = jnp.stack([attn_gain_sum, out_rows[:, model_width + EXPERTS]], axis=1)

    square_total = (
        jnp.sum(qkv_sum * qkv_sum)
        + jnp.sum(out_sum * out_sum)
        + jnp.sum(router_sum * router_sum)
        + jnp.sum(in_sum * in_sum)
        + jnp.sum(down_sum * down_sum)
        + jnp.sum(gains_sum * gains_sum)
    )
    grad_norm = jnp.sqrt(total_over(square_total))
    factor = CLIP_NORM / jnp.maximum(grad_norm, CLIP_NORM)
    new_weights, new_moments, new_seconds = update_all(
        (query_key_value_weight, out_weight, router_weight, expert_in, expert_down, norm_gains),
        (qkv_sum, out_sum, router_sum, in_sum, down_sum, gains_sum),
        (query_key_value_moment, out_moment, router_moment, in_moment, down_moment, gains_moment),
        (query_key_value_second, out_second, router_second, in_second, down_second, gains_second),
        factor,
    )
    return (
        output[None],
        input_grad.astype(BF16)[None],
        grad_norm,
        *new_weights,
        *new_moments,
        *new_seconds,
    )


def solution(mesh):
    mesh = jax.sharding.Mesh(
        mesh.devices.reshape(mesh.shape["seq"], mesh.shape["fsdp"] // 4, 2, 2), ALL_AXES
    )
    token_spec = P(ROWS, "x", None)
    row_spec = P(ALL_AXES, None)
    expert_spec = P(None, ALL_AXES, None)
    state_specs = (row_spec, row_spec, row_spec, expert_spec, expert_spec, row_spec)
    return jax.shard_map(
        shards,
        mesh=mesh,
        in_specs=(token_spec, token_spec, P(ROWS, "x"), token_spec) + state_specs * 3,
        out_specs=(token_spec, token_spec, P()) + state_specs * 3,
        check_vma=False,
    )
```

```python
import functools
import itertools

import jax
import jax.numpy as jnp
from jax import lax
from jax.experimental import pallas as pl
from jax.experimental.pallas import tpu as pltpu
from jax.sharding import PartitionSpec as P

MODEL_DIMENSION = 1536
QUERY_HEADS = 12
KEY_VALUE_HEADS = 2
HEAD_DIMENSION = 128
F = 768
EXPERTS = 8
TOPK = 4
STEP = 10
CAP = 320


PRECISE = lax.Precision.HIGHEST
NORM_EPS = 1e-06
CLIP_NORM = 1.0
BETA_ONE = 0.9
BETA_TWO = 0.95
ADAM_EPS = 1e-08
DECAY_RATE = 0.1
ROPE_BASE = 10000.0
MASKED_SCORE = -1e30

F32 = jnp.float32
BF16 = jnp.bfloat16
ALL_AXES = ("x", "z", "y", "core")
ROWS = ("z", "y", "core")
SOURCES = 4
OWN_EXPERTS = EXPERTS // SOURCES
Z_STEPS = 4
LANES = 128
MIB = 1024 * 1024
COST_SCALE = 4


def cost(flops, bytes_accessed, transcendentals=0):
    return pl.CostEstimate(
        flops=flops // COST_SCALE,
        bytes_accessed=bytes_accessed // COST_SCALE,
        transcendentals=transcendentals // COST_SCALE,
    )


def rms_scale(values):
    return lax.rsqrt(jnp.mean(values * values, axis=-1, keepdims=True) + NORM_EPS)


def step_sizes():
    return (
        MODEL_DIMENSION ** (-0.5),
        (QUERY_HEADS * HEAD_DIMENSION // 64) ** (-0.5),
        (4 * MODEL_DIMENSION) ** (-0.5),
        MODEL_DIMENSION ** (-0.5),
        (F // 64) ** (-0.5),
        0.3,
    )


def adam_step(weight, gradient, moment, second, step_size, decay_value):
    moment_new = BETA_ONE * moment + (1.0 - BETA_ONE) * gradient
    second_new = BETA_TWO * second + (1.0 - BETA_TWO) * gradient * gradient
    corrected = (
        moment_new
        / (1.0 - BETA_ONE**STEP)
        / (jnp.sqrt(second_new / (1.0 - BETA_TWO**STEP)) + ADAM_EPS)
    )
    return (weight - step_size * (corrected + decay_value * weight), moment_new, second_new)


def update_all(weights, gradients, moments, seconds, factor):
    sizes_list = step_sizes()
    decays = (DECAY_RATE, DECAY_RATE, DECAY_RATE, DECAY_RATE, DECAY_RATE, 0.0)
    new_weights = []
    new_moments = []
    new_seconds = []
    for position in range(6):
        weight_new, moment_new, second_new = adam_step(
            weights[position],
            gradients[position] * factor,
            moments[position],
            seconds[position],
            sizes_list[position],
            decays[position],
        )
        new_weights.append(weight_new)
        new_moments.append(moment_new)
        new_seconds.append(second_new)
    return (new_weights, new_moments, new_seconds)


def norm_value_grad(values, norm_scale, gain_row, upstream):
    scaled = gain_row * upstream
    return norm_scale * scaled - values * norm_scale**3 * jnp.mean(
        values * scaled, axis=-1, keepdims=True
    )


def dot_nt(a, b):
    return lax.dot_general(a, b, (((1,), (1,)), ((), ())), preferred_element_type=F32)


def dot_tn(a, b):
    return lax.dot_general(a, b, (((0,), (0,)), ((), ())), preferred_element_type=F32)


def swap(value, axis):
    return lax.ppermute(value, axis, [(0, 1), (1, 0)])


def rotate(value, step):
    size = lax.axis_size("z")
    return lax.ppermute(value, "z", [(i, (i + step) % size) for i in range(size)])


def hold(values, *others):
    count = len(values)
    spec = pl.BlockSpec(memory_space=pl.ANY)
    return pl.pallas_call(
        lambda *refs: None,
        in_specs=[spec] * (count + len(others)),
        out_specs=[spec] * count,
        out_shape=[jax.ShapeDtypeStruct(v.shape, v.dtype) for v in values],
        input_output_aliases={i: i for i in range(count)},
        name="hold",
    )(*values, *others)


def by_index(index, own, other):
    return jnp.where(index == 0, jnp.stack([own, other]), jnp.stack([other, own]))


def take_index(index, array, axis):
    return lax.dynamic_index_in_dim(array, index, axis=axis, keepdims=False)


def total_over(value):
    if lax.axis_size("z") != Z_STEPS:
        return lax.psum(value, ALL_AXES)
    value = jnp.broadcast_to(value, (8, LANES))
    value = value + sum(rotate(value, k) for k in range(1, Z_STEPS))
    for axis in ("x", "y", "core"):
        value = value + swap(value, axis)
    return value[0, 0]


def place():
    return jnp.stack([lax.axis_index(a) for a in ALL_AXES]).astype(jnp.int32)


def block_of(place_ref, rel_x, rel_z, rel_y):
    x = lax.rem(place_ref[0] + rel_x, 2)
    z = lax.rem(place_ref[1] + rel_z, Z_STEPS)
    y = lax.rem(place_ref[2] + rel_y, 2)
    return (x * Z_STEPS + z) * 2 + y


def row_blocks():
    return [
        (c, y, x, z) for c in range(2) for y in range(2) for x in range(2) for z in range(Z_STEPS)
    ]


def row_copies(place_ref, own_ref, other_ref, targets, sems, first):
    rows = own_ref.shape[-2]
    copies = []
    for c, y, x, z in row_blocks():
        core = lax.rem(place_ref[3] + c, 2)
        row = pl.multiple_of((block_of(place_ref, x, z, y) * 2 + core) * rows, rows)
        for start, width, ref, column in targets:
            copies.append(
                pltpu.make_async_copy(
                    (own_ref, other_ref)[c].at[y, x, z, :, pl.ds(start, width)],
                    ref.at[pl.ds(row, rows), pl.ds(column, width)],
                    sems.at[first + len(copies)],
                )
            )
    return copies


def gather_whole(shard):
    whole = lax.all_gather(shard, ALL_AXES, axis=0, tiled=True)
    blocks = whole.reshape(2, Z_STEPS, 2, 2, -1, whole.shape[1])
    blocks = jnp.transpose(blocks, (3, 2, 0, 1, 4, 5))
    return blocks[0], blocks[1]


def scatter_whole(keep, send):
    blocks = jnp.transpose(jnp.stack([keep, send]), (2, 3, 1, 0, 4, 5))
    return lax.psum_scatter(
        blocks.reshape(-1, blocks.shape[-1]), ALL_AXES, scatter_dimension=0, tiled=True
    ).astype(F32)


def grad_rows_kernel(count, has_extra, edges, place_ref, a_ref, *rest):
    rest = list(rest)
    b_refs = [rest.pop(0) for _ in range(count)]
    extra_ref = rest.pop(0) if has_extra else None
    outs = [(rest.pop(0), rest.pop(0)) for _ in edges[1:]]
    held, sems = rest
    rows = outs[0][0].shape[-2]

    @pl.loop(0, a_ref.shape[1] // 256)
    def _(i):
        tile = pl.ds(pl.multiple_of(i * 256, 256), 256)
        start = 0
        for b_ref in b_refs:
            grad = dot_tn(a_ref[:, tile], b_ref[...])
            held[tile, pl.ds(start, b_ref.shape[1])] = grad.astype(BF16)
            start += b_ref.shape[1]

    if has_extra:
        held[:, pl.ds(held.shape[1] - LANES, LANES)] = extra_ref[...].astype(BF16)
    copies = []
    for pair, start, end in zip(outs, edges, edges[1:]):
        for c, y, x, z in row_blocks():
            core = lax.rem(place_ref[3] + c, 2)
            row = pl.multiple_of((block_of(place_ref, x, z, y) * 2 + core) * rows, rows)
            copies.append(
                pltpu.make_async_copy(
                    held.at[pl.ds(row, rows), pl.ds(start, end - start)],
                    pair[c].at[y, x, z],
                    sems.at[len(copies)],
                )
            )
    for copy in copies:
        copy.start()
    for copy in copies:
        copy.wait()


def grad_rows(where, a, bs, extra, edges):
    model_rows = a.shape[1]
    rows = model_rows // (2 * Z_STEPS * 2 * 2)
    width = edges[-1]
    any_spec = pl.BlockSpec(memory_space=pl.ANY)
    vmem_spec = pl.BlockSpec(memory_space=pltpu.VMEM)
    operands = (a, *bs) + (() if extra is None else (extra,))
    parts = len(edges) - 1
    outs = pl.pallas_call(
        functools.partial(grad_rows_kernel, len(bs), extra is not None, edges),
        grid_spec=pltpu.PrefetchScalarGridSpec(
            num_scalar_prefetch=1,
            grid=(1,),
            in_specs=[vmem_spec] * len(operands),
            out_specs=[any_spec] * (2 * parts),
            scratch_shapes=[
                pltpu.VMEM((model_rows, width), BF16),
                pltpu.SemaphoreType.DMA((len(row_blocks()) * parts,)),
            ],
        ),
        out_shape=[
            jax.ShapeDtypeStruct((2, 2, Z_STEPS, rows, end - start), BF16)
            for start, end in zip(edges, edges[1:])
            for _ in range(2)
        ],
        compiler_params=pltpu.CompilerParams(vmem_limit_bytes=48 * MIB),
        cost_estimate=cost(
            4 * a.shape[0] * model_rows * width, 4 * model_rows * width
        ),
        name="grad_rows",
    )(where, *operands)
    return [(outs[2 * i], outs[2 * i + 1]) for i in range(parts)]


def kept_sent(blocks, axis):
    at = 0 if axis == "y" or blocks.ndim == 4 else 1
    return [lax.index_in_dim(blocks, i, axis=at, keepdims=False) for i in range(2)]


def fold(kept, sent, axis):
    return kept.astype(F32) + swap(sent.astype(BF16), axis).astype(F32)


def rotated(values, cosine, sine):
    return values * cosine + pltpu.roll(values, HEAD_DIMENSION // 2, 1) * sine


def project_kernel(
    place_ref,
    x_ref,
    own,
    other,
    cos_ref,
    sin_ref,
    query_ref,
    kv_ref,
    normed_ref,
    weight_out,
    small_out,
    weight,
    small,
    sems,
    out_sems,
):
    step = pl.program_id(0)
    columns = weight.shape[1]
    keep = [
        pltpu.make_async_copy(weight, weight_out, out_sems.at[0]),
        pltpu.make_async_copy(small, small_out, out_sems.at[1]),
    ]

    @pl.when(step == 0)
    def _():
        copies = row_copies(
            place_ref,
            own,
            other,
            ((0, columns, weight, 0), (columns, LANES, small, 0)),
            sems,
            0,
        )
        for copy in copies:
            copy.start()
        for copy in copies:
            copy.wait()
        for copy in keep:
            copy.start()
        gain = small[...].astype(F32).T[EXPERTS : EXPERTS + 1, :]
        values = x_ref[...].astype(F32)
        normed_ref[...] = (values * rms_scale(values) * gain).astype(BF16)

    tile = KEY_VALUE_HEADS * HEAD_DIMENSION
    at = pl.ds(pl.multiple_of(step * tile, tile), tile)
    mixed = jnp.dot(normed_ref[...], weight[:, at], preferred_element_type=F32)
    query_steps = pl.num_programs(0) - 2

    def turned():
        return jnp.concatenate(
            [
                rotated(
                    mixed[:, h * HEAD_DIMENSION : (h + 1) * HEAD_DIMENSION],
                    cos_ref[...],
                    sin_ref[...],
                ).astype(BF16)
                for h in range(KEY_VALUE_HEADS)
            ],
            axis=1,
        )

    @pl.when(step < query_steps)
    def _():
        query_ref[...] = turned()

    @pl.when(step == query_steps)
    def _():
        kv_ref[...] = turned()

    @pl.when(step == query_steps + 1)
    def _():
        kv_ref[...] = mixed.astype(BF16)
        for copy in keep:
            copy.wait()


def project(where, x, pair, cosine, sine):
    rows, depth = x.shape
    columns = pair[0].shape[-1] - LANES
    tile = KEY_VALUE_HEADS * HEAD_DIMENSION
    query_steps = QUERY_HEADS // KEY_VALUE_HEADS
    whole = lambda i, *_: (0, 0)
    any_spec = pl.BlockSpec(memory_space=pl.ANY)
    turn = pl.BlockSpec((rows, HEAD_DIMENSION), whole)
    return pl.pallas_call(
        project_kernel,
        grid_spec=pltpu.PrefetchScalarGridSpec(
            num_scalar_prefetch=1,
            grid=(query_steps + 2,),
            in_specs=[pl.BlockSpec((rows, depth), whole)] + [any_spec] * 2 + [turn] * 2,
            out_specs=[
                pl.BlockSpec((rows, tile), lambda i, *_: (0, jnp.minimum(i, query_steps - 1))),
                pl.BlockSpec((rows, tile), lambda i, *_: (0, jnp.maximum(i - query_steps, 0))),
                pl.BlockSpec((rows, depth), whole),
                any_spec,
                any_spec,
            ],
            scratch_shapes=[
                pltpu.VMEM((depth, columns), BF16),
                pltpu.VMEM((depth, LANES), BF16),
                pltpu.SemaphoreType.DMA((2 * len(row_blocks()),)),
                pltpu.SemaphoreType.DMA((2,)),
            ],
        ),
        out_shape=[
            jax.ShapeDtypeStruct((rows, query_steps * tile), BF16),
            jax.ShapeDtypeStruct((rows, 2 * tile), BF16),
            jax.ShapeDtypeStruct((rows, depth), BF16),
            jax.ShapeDtypeStruct((depth, columns), BF16),
            jax.ShapeDtypeStruct((depth, LANES), BF16),
        ],
        compiler_params=pltpu.CompilerParams(vmem_limit_bytes=40 * MIB),
        cost_estimate=cost(
            6 * rows * depth * columns, 20 * MIB
        ),
        name="project",
    )(where, x, *pair, cosine, sine)


def join_kernel(
    place_ref,
    attended_ref,
    x_ref,
    gain_ref,
    own,
    other,
    middle_ref,
    normed_ref,
    scale_ref,
    weight_out,
    weight,
    sems,
    out_sems,
):
    copies = row_copies(place_ref, own, other, ((0, weight.shape[1], weight, 0),), sems, 0)
    for copy in copies:
        copy.start()
    for copy in copies:
        copy.wait()
    keep = pltpu.make_async_copy(weight, weight_out, out_sems.at[0])
    keep.start()
    wide = 512
    width = weight.shape[1]

    def join(i, total):
        at = pl.ds(pl.multiple_of(i * wide, wide), wide)
        middle = x_ref[:, at].astype(F32) + jnp.dot(
            attended_ref[...], weight[:, at], preferred_element_type=F32
        )
        middle_ref[:, at] = middle
        return total + jnp.sum(middle * middle, axis=1, keepdims=True)

    total = lax.fori_loop(0, width // wide, join, jnp.zeros((x_ref.shape[0], 1), F32))
    scale = lax.rsqrt(total / width + NORM_EPS)
    scale_ref[...] = scale
    normed_ref[...] = (middle_ref[...] * scale * gain_ref[...]).astype(BF16)
    keep.wait()


def join(where, attended, x, gain, pair):
    rows, depth = attended.shape
    width = pair[0].shape[-1]
    any_spec = pl.BlockSpec(memory_space=pl.ANY)
    vmem_spec = pl.BlockSpec(memory_space=pltpu.VMEM)
    return pl.pallas_call(
        join_kernel,
        grid_spec=pltpu.PrefetchScalarGridSpec(
            num_scalar_prefetch=1,
            grid=(1,),
            in_specs=[vmem_spec] * 3 + [any_spec] * 2,
            out_specs=[vmem_spec] * 3 + [any_spec],
            scratch_shapes=[
                pltpu.VMEM((depth, width), BF16),
                pltpu.SemaphoreType.DMA((len(row_blocks()),)),
                pltpu.SemaphoreType.DMA((1,)),
            ],
        ),
        out_shape=[
            jax.ShapeDtypeStruct((rows, width), F32),
            jax.ShapeDtypeStruct((rows, width), BF16),
            jax.ShapeDtypeStruct((rows, 1), F32),
            jax.ShapeDtypeStruct((depth, width), BF16),
        ],
        compiler_params=pltpu.CompilerParams(vmem_limit_bytes=40 * MIB),
        cost_estimate=cost(
            4 * rows * depth * width, 16 * MIB
        ),
        name="join",
    )(where, attended, x, gain, *pair)


def score_pair(q, ko_ref, kp_ref, seg_col, seg_own, seg_prev):
    scale = HEAD_DIMENSION ** (-0.5)
    own = dot_nt(q, ko_ref[...]) * scale
    query_at = lax.broadcasted_iota(jnp.int32, own.shape, 0)
    key_at = lax.broadcasted_iota(jnp.int32, own.shape, 1)
    own = jnp.where((seg_col == seg_own) & (key_at <= query_at), own, MASKED_SCORE)
    if kp_ref is None:
        return (own,)
    prev = dot_nt(q, kp_ref[...]) * scale
    return (own, jnp.where(seg_col == seg_prev, prev, MASKED_SCORE))


def attend_kernel(
    half_ref, q_ref, ko_ref, vo_ref, kp_ref, vp_ref, sc_ref, so_ref, sp_ref, out_ref, log_ref
):
    def run(with_previous):
        parts = score_pair(
            q_ref[...],
            ko_ref,
            kp_ref if with_previous else None,
            sc_ref[...],
            so_ref[...],
            sp_ref[...],
        )
        highest = jnp.max(parts[0], axis=-1, keepdims=True)
        for part in parts[1:]:
            highest = jnp.maximum(highest, jnp.max(part, axis=-1, keepdims=True))
        exponents = [jnp.exp(part - highest) for part in parts]
        total = sum(jnp.sum(part, axis=-1, keepdims=True) for part in exponents)
        scale = 1.0 / total
        mixed = sum(
            jnp.dot((part * scale).astype(BF16), ref[...], preferred_element_type=F32)
            for part, ref in zip(exponents, (vo_ref, vp_ref))
        )
        out_ref[...] = mixed.astype(BF16)
        log_ref[0] = highest + jnp.log(total)

    pl.when(half_ref[0] == 0)(lambda: run(False))
    pl.when(half_ref[0] != 0)(lambda: run(True))


def head_specs(rows):
    group = QUERY_HEADS // KEY_VALUE_HEADS
    query = pl.BlockSpec((rows, HEAD_DIMENSION), lambda h, *_: (0, h))
    key = pl.BlockSpec((rows, HEAD_DIMENSION), lambda h, *_: (0, h // group))
    value = pl.BlockSpec((rows, HEAD_DIMENSION), lambda h, *_: (0, KEY_VALUE_HEADS + h // group))
    col = pl.BlockSpec((rows, 1), lambda h, *_: (0, 0))
    row = pl.BlockSpec((1, rows), lambda h, *_: (0, 0))
    log = pl.BlockSpec((1, rows, 1), lambda h, *_: (h, 0, 0))
    return query, [query, key, value, key, value, col, row, row], log


def attend(queries, own, previous, seg_col, seg_own, seg_prev, half):
    rows = queries.shape[0]
    query, specs, log = head_specs(rows)
    return pl.pallas_call(
        attend_kernel,
        grid_spec=pltpu.PrefetchScalarGridSpec(
            num_scalar_prefetch=1,
            grid=(QUERY_HEADS,),
            in_specs=specs,
            out_specs=[query, log],
        ),
        out_shape=[
            jax.ShapeDtypeStruct((rows, QUERY_HEADS * HEAD_DIMENSION), BF16),
            jax.ShapeDtypeStruct((QUERY_HEADS, rows, 1), F32),
        ],
        compiler_params=pltpu.CompilerParams(vmem_limit_bytes=40 * MIB),
        cost_estimate=cost(
            8 * rows * rows * QUERY_HEADS * HEAD_DIMENSION, 16 * MIB, 2 * rows * rows * QUERY_HEADS
        ),
        name="attend",
    )(half, queries, own, own, previous, previous, seg_col, seg_own, seg_prev)


def attend_back_kernel(
    half_ref,
    q_ref,
    ko_ref,
    vo_ref,
    kp_ref,
    vp_ref,
    sc_ref,
    so_ref,
    sp_ref,
    up_ref,
    log_ref,
    cos_ref,
    sin_ref,
    dq_ref,
    dko_ref,
    dvo_ref,
    dkp_ref,
    dvp_ref,
):
    scale = HEAD_DIMENSION ** (-0.5)
    first = lax.rem(pl.program_id(0), QUERY_HEADS // KEY_VALUE_HEADS) == 0

    @pl.when(first)
    def _():
        for ref in (dko_ref, dvo_ref, dkp_ref, dvp_ref):
            ref[...] = jnp.zeros_like(ref)

    def run(with_previous):
        q, up = q_ref[...], up_ref[...]
        parts = score_pair(
            q, ko_ref, kp_ref if with_previous else None, sc_ref[...], so_ref[...], sp_ref[...]
        )
        weights = [jnp.exp(part - log_ref[0]) for part in parts]
        grads = [dot_nt(up, ref[...]) for ref, _ in zip((vo_ref, vp_ref), parts)]
        inner = sum(
            jnp.sum(w * g, axis=-1, keepdims=True) for w, g in zip(weights, grads)
        )
        scores = [(w * (g - inner)).astype(BF16) for w, g in zip(weights, grads)]
        dq = sum(
            jnp.dot(s, ref[...], preferred_element_type=F32)
            for s, ref in zip(scores, (ko_ref, kp_ref))
        )
        dq = (dq * scale).astype(BF16).astype(F32)
        dq_ref[...] = rotated(dq, cos_ref[...], sin_ref[...]).astype(BF16)
        for s, w, dk_ref, dv_ref in zip(scores, weights, (dko_ref, dkp_ref), (dvo_ref, dvp_ref)):
            dk_ref[...] += dot_tn(s, q) * scale
            dv_ref[...] += dot_tn(w.astype(BF16), up)

    pl.when(half_ref[0] == 0)(lambda: run(False))
    pl.when(half_ref[0] != 0)(lambda: run(True))


def attend_back(queries, own, previous, seg_col, seg_own, seg_prev, half, up, log_sums, cosine, sine):
    rows = queries.shape[0]
    query, specs, log = head_specs(rows)
    group = QUERY_HEADS // KEY_VALUE_HEADS
    turn = pl.BlockSpec((rows, HEAD_DIMENSION), lambda h, *_: (0, 0))
    kv = pl.BlockSpec((rows, HEAD_DIMENSION), lambda h, *_: (0, h // group))
    kv_shape = jax.ShapeDtypeStruct((rows, KEY_VALUE_HEADS * HEAD_DIMENSION), F32)
    return pl.pallas_call(
        attend_back_kernel,
        grid_spec=pltpu.PrefetchScalarGridSpec(
            num_scalar_prefetch=1,
            grid=(QUERY_HEADS,),
            in_specs=specs + [query, log, turn, turn],
            out_specs=[query, kv, kv, kv, kv],
        ),
        out_shape=[jax.ShapeDtypeStruct((rows, QUERY_HEADS * HEAD_DIMENSION), BF16)]
        + [kv_shape] * 4,
        compiler_params=pltpu.CompilerParams(vmem_limit_bytes=48 * MIB),
        cost_estimate=cost(
            20 * rows * rows * QUERY_HEADS * HEAD_DIMENSION, 24 * MIB, 2 * rows * rows * QUERY_HEADS
        ),
        name="attend_back",
    )(
        half,
        queries,
        own,
        own,
        previous,
        previous,
        seg_col,
        seg_own,
        seg_prev,
        up,
        log_sums,
        cosine,
        sine,
    )


def expert_kernel(count, given, gives, grads_too, place_ref, *refs):
    refs = list(refs)
    pop = lambda n: [refs.pop(0) for _ in range(n)]
    pieces = pop(4)
    x_refs, t_refs = pop(count), pop(count)
    rank_row_ref, rank_col_ref, router_ref = pop(3)
    given_refs = pop(4) if given else []
    mix_refs, ffn_refs = pop(count), pop(count)
    (gate_grad_ref,) = pop(1)
    gives_refs = pop(4) if gives else []
    grads = pop(4) if grads_too else []
    (
        in_w,
        down_w,
        picked,
        joined_grad,
        active,
        slot_grad,
        top,
        spread,
        gates,
        x_held,
        t_held,
        sems,
        token_sems,
        given_sems,
    ) = refs
    in_rows = in_w.shape[0] // (4 * Z_STEPS)
    down_rows = down_w.shape[0] // (4 * Z_STEPS)
    tokens, width = x_refs[0].shape
    hidden = active.shape[1]
    slots = count * CAP
    own_slots = pl.ds(0, slots)
    wide, narrow = 512, 256

    def block_copies(outward, which):
        copies = []
        for (y, x), piece in zip(
            itertools.product(range(2), range(2)), grads if outward else pieces
        ):
            for z in range(Z_STEPS):
                block = (lax.rem(place_ref[0] + x, 2) * Z_STEPS + z) * 2 + lax.rem(
                    place_ref[2] + y, 2
                )
                whole, rows, start = (
                    (in_w, in_rows, 0) if which == 0 else (down_w, down_rows, in_rows)
                )
                ends = (
                    piece.at[z, pl.ds(start, rows), :],
                    whole.at[pl.ds(pl.multiple_of(block * rows, rows), rows), :],
                )
                if outward:
                    ends = ends[::-1]
                copies.append(pltpu.make_async_copy(*ends, sems.at[which, len(copies)]))
        return copies

    def token_copies(s):
        return [
            pltpu.make_async_copy(many[s], held.at[s % 2], token_sems.at[i, s % 2])
            for i, (many, held) in enumerate(((x_refs, x_held), (t_refs, t_held)))
        ]

    kept = (picked, joined_grad, active, slot_grad)
    arriving = [
        pltpu.make_async_copy(
            ref, held.at[pl.ds(slots, held.shape[0] - slots), :], given_sems.at[i]
        )
        for i, (ref, held) in enumerate(zip(given_refs, kept))
    ]
    leaving = [
        pltpu.make_async_copy(held.at[own_slots, :], ref, given_sems.at[i])
        for i, (ref, held) in enumerate(zip(gives_refs, kept))
    ]
    weight_copies = block_copies(False, 0) + block_copies(False, 1)
    for copy in token_copies(0) + weight_copies + arriving:
        copy.start()

    for s in range(count):
        for copy in token_copies(s):
            copy.wait()
        if s + 1 < count:
            for copy in token_copies(s + 1):
                copy.start()
        at_slots = slice(s * CAP, (s + 1) * CAP)
        chosen = (
            lax.broadcasted_iota(jnp.int32, (CAP, tokens), 0) == rank_row_ref[s]
        ).astype(F32)
        spread[s] = (
            (lax.broadcasted_iota(jnp.int32, (tokens, CAP), 1) == rank_col_ref[s])
            .astype(F32)
            .astype(BF16)
        )
        expert_row = lax.broadcasted_iota(jnp.int32, (router_ref.shape[0], tokens), 0)
        logits = jnp.where(
            expert_row < EXPERTS, dot_nt(router_ref[...], x_held[s % 2]), MASKED_SCORE
        )
        exponent = jnp.exp(logits - jnp.max(logits, axis=0, keepdims=True))
        probs = exponent / jnp.sum(exponent, axis=0, keepdims=True)
        gate_row = jnp.sum(
            jnp.where(expert_row == place_ref[4], probs, 0.0), axis=0, keepdims=True
        )
        gate = jnp.sum(chosen * gate_row, axis=1, keepdims=True)
        gates[at_slots, :] = gate
        pick = chosen.astype(BF16)

        @pl.loop(0, width // wide)
        def _(i, s=s, pick=pick, gate=gate, at_slots=at_slots):
            at = pl.ds(pl.multiple_of(i * wide, wide), wide)
            picked[at_slots, at] = jnp.dot(
                pick, x_held[s % 2, :, at], preferred_element_type=F32
            ).astype(BF16)
            top_rows = jnp.dot(pick, t_held[s % 2, :, at], preferred_element_type=F32)
            top[at_slots, at] = top_rows.astype(BF16)
            slot_grad[at_slots, at] = (gate * top_rows).astype(BF16)

    for copy in weight_copies:
        copy.wait()

    @pl.loop(0, hidden // narrow)
    def _(i):
        at = pl.ds(pl.multiple_of(i * narrow, narrow), narrow)
        up_at = pl.ds(pl.multiple_of(hidden + i * narrow, narrow), narrow)
        rows = picked[own_slots, :]
        gate_part = jnp.dot(rows, in_w[:, at], preferred_element_type=F32)
        up_part = jnp.dot(rows, in_w[:, up_at], preferred_element_type=F32)
        act_grad = dot_nt(slot_grad[own_slots, :], down_w[at, :])
        sigmoid = jax.nn.sigmoid(gate_part)
        silu = gate_part * sigmoid
        active[own_slots, at] = (silu * up_part).astype(BF16)
        joined_grad[own_slots, at] = (
            act_grad * up_part * sigmoid * (1.0 + gate_part * (1.0 - sigmoid))
        ).astype(BF16)
        joined_grad[own_slots, up_at] = (act_grad * silu).astype(BF16)

    for copy in leaving:
        copy.start()

    def results(i, total):
        at = pl.ds(pl.multiple_of(i * wide, wide), wide)
        result = jnp.dot(active[own_slots, :], down_w[:, at], preferred_element_type=F32)
        mix = (gates[...] * result).astype(BF16)
        back = dot_nt(joined_grad[own_slots, :], in_w[at, :]).astype(BF16)
        for s in range(count):
            at_slots = slice(s * CAP, (s + 1) * CAP)
            for rows, out in ((mix, mix_refs[s]), (back, ffn_refs[s])):
                out[:, at] = jnp.dot(
                    spread[s], rows[at_slots], preferred_element_type=F32
                ).astype(BF16)
        return total + jnp.sum(result * top[:, at].astype(F32), axis=1, keepdims=True)

    gate_grad = lax.fori_loop(0, width // wide, results, jnp.zeros((slots, 1), F32))
    for s in range(count):
        chosen = lax.broadcasted_iota(jnp.int32, (CAP, tokens), 0) == rank_row_ref[s]
        gate_grad_ref[s] = jnp.sum(
            jnp.where(chosen, gate_grad[s * CAP : (s + 1) * CAP], 0.0), axis=0, keepdims=True
        )
    for copy in arriving + leaving:
        copy.wait()

    if grads_too:
        down_w[...] = dot_tn(active[...], slot_grad[...]).astype(BF16)

        down_copies = block_copies(True, 1)
        for copy in down_copies:
            copy.start()

        @pl.loop(0, width // hidden)
        def _(i):
            at = pl.ds(pl.multiple_of(i * hidden, hidden), hidden)
            in_w[at, :] = dot_tn(picked[:, at], joined_grad[...]).astype(BF16)

        in_copies = block_copies(True, 0)
        for copy in in_copies:
            copy.start()
        for copy in down_copies + in_copies:
            copy.wait()


def expert_pass(where, pieces, x_some, t_some, rank, router_rows, given, gives, grads_too):
    count = len(x_some)
    tokens, width = x_some[0].shape
    hidden = F
    slots = count * CAP
    held_slots = slots + (given[0].shape[0] if given else 0)
    any_spec = pl.BlockSpec(memory_space=pl.ANY)
    vmem_spec = pl.BlockSpec(memory_space=pltpu.VMEM)
    token_shape = jax.ShapeDtypeStruct((tokens, width), BF16)
    kept_widths = (width, 2 * hidden, hidden, width)
    flops = 2 * slots * width * hidden * 9 + 8 * slots * tokens * width
    outs = pl.pallas_call(
        functools.partial(expert_kernel, count, bool(given), gives, grads_too),
        grid_spec=pltpu.PrefetchScalarGridSpec(
            num_scalar_prefetch=1,
            grid=(1,),
            in_specs=[any_spec] * (len(pieces) + 2 * count)
            + [vmem_spec] * 3
            + [any_spec] * len(given),
            out_specs=[vmem_spec] * (2 * count + 1)
            + [any_spec] * (4 * gives + 4 * grads_too),
            scratch_shapes=[
                pltpu.VMEM((width, 2 * hidden), BF16),
                pltpu.VMEM((hidden, width), BF16),
                pltpu.VMEM((held_slots, width), BF16),
                pltpu.VMEM((held_slots, 2 * hidden), BF16),
                pltpu.VMEM((held_slots, hidden), BF16),
                pltpu.VMEM((held_slots, width), BF16),
                pltpu.VMEM((slots, width), BF16),
                pltpu.VMEM((count, tokens, CAP), BF16),
                pltpu.VMEM((slots, 1), F32),
                pltpu.VMEM((2, tokens, width), BF16),
                pltpu.VMEM((2, tokens, width), BF16),
                pltpu.SemaphoreType.DMA((2, 4 * Z_STEPS)),
                pltpu.SemaphoreType.DMA((2, 2)),
                pltpu.SemaphoreType.DMA((4,)),
            ],
        ),
        out_shape=[token_shape] * (2 * count)
        + [jax.ShapeDtypeStruct((count, 1, tokens), F32)]
        + [jax.ShapeDtypeStruct((slots, w), BF16) for w in kept_widths if gives]
        + [jax.ShapeDtypeStruct(p.shape, BF16) for p in pieces if grads_too],
        compiler_params=pltpu.CompilerParams(vmem_limit_bytes=60 * MIB),
        cost_estimate=cost(
            8 * flops, 96 * MIB, slots * hidden
        ),
        name="expert",
    )(where, *pieces, *x_some, *t_some, *rank, router_rows, *given)
    rest = list(outs[2 * count + 1 :])
    kept = [rest.pop(0) for _ in range(4 * gives)]
    return outs[:count], outs[count : 2 * count], outs[2 * count], kept, rest


def expert_pairs(expert_in, expert_down):
    core = lax.axis_index("core")
    low = jnp.concatenate([expert_in.astype(BF16), expert_down.astype(BF16)], axis=1)
    low = low.reshape(2, 2, OWN_EXPERTS, *low.shape[1:])
    return by_index(core, take_index(core, low, 1), swap(take_index(1 - core, low, 1), "core"))


def expert_halves(pair, number, in_rows):
    x = lax.axis_index("x")
    pair = pair[:, :, number]
    width = pair.shape[-1]
    both = jnp.concatenate(
        [
            jnp.swapaxes(part, 0, 1).reshape(2, -1, width)
            for part in (pair[:, :, :in_rows], pair[:, :, in_rows:])
        ],
        axis=1,
    )
    return take_index(x, both, 0), take_index(1 - x, both, 0)


def gather_expert_whole(pair, number, in_rows):
    own, sent = expert_halves(pair, number, in_rows)
    chunk = by_index(lax.axis_index("x"), own, swap(sent, "x"))
    whole = lax.all_gather(chunk, ("z", "y"))
    rows = chunk.shape[1] * 2 // 3
    width = chunk.shape[2]
    parts = [
        jnp.moveaxis(part, 0, 1).reshape(2, Z_STEPS, 2, -1, width)
        for part in (whole[:, :, :rows], whole[:, :, rows:])
    ]
    both = jnp.concatenate(parts, axis=3)
    return [both[x, :, y] for y in range(2) for x in range(2)]


def scatter_expert_whole(grads):
    spots = lax.axis_size("z") * 2
    both = jnp.stack(grads).reshape((2, 2) + grads[0].shape)
    both = jnp.transpose(both, (1, 2, 0, 3, 4))
    width = both.shape[-1]
    in_rows = both.shape[3] * 2 // 3
    parts = [
        part.reshape(2, spots, -1, width)
        for part in (both[:, :, :, :in_rows], both[:, :, :, in_rows:])
    ]
    both = jnp.moveaxis(jnp.concatenate(parts, axis=2), 1, 0)
    total = lax.psum_scatter(both, ("z", "y"), scatter_dimension=0)
    x = lax.axis_index("x")
    return take_index(x, total, 0), take_index(1 - x, total, 0)


def finish_expert(sums, in_rows):
    x, core = lax.axis_index("x"), lax.axis_index("core")
    width = sums[0].shape[-1]
    both = by_index(x, sums[0], swap(sums[1], "x"))
    split = jnp.concatenate(
        [
            both[:, : 2 * in_rows].reshape(2, 2, in_rows, width),
            both[:, 2 * in_rows :].reshape(2, 2, -1, width),
        ],
        axis=2,
    )
    other = swap(take_index(1 - core, split, 1), "core")
    both = jnp.swapaxes(by_index(core, take_index(core, split, 1), other), 0, 1).astype(F32)
    return both[:, :, :in_rows], both[:, :, in_rows:]


def shards(
    tokens,
    cotangent,
    segment_ids,
    route_ids,
    query_key_value_weight,
    out_weight,
    router_weight,
    expert_in,
    expert_down,
    norm_gains,
    query_key_value_moment,
    out_moment,
    router_moment,
    in_moment,
    down_moment,
    gains_moment,
    query_key_value_second,
    out_second,
    router_second,
    in_second,
    down_second,
    gains_second,
):
    local_rows = tokens.shape[1]
    model_width = tokens.shape[2]
    staged = lax.axis_size("z") == Z_STEPS
    x_index = lax.axis_index("x")
    shard_rows = query_key_value_weight.shape[0]
    in_rows, down_rows = expert_in.shape[1], expert_down.shape[1]
    key_width = KEY_VALUE_HEADS * HEAD_DIMENSION
    first_expert = (x_index * 2 + lax.axis_index("core")) * OWN_EXPERTS
    where = place() if staged else jnp.zeros((4,), jnp.int32)
    x_tokens, top = tokens[0], cotangent[0]

    own_gains = norm_gains.astype(BF16)
    small_part = jnp.concatenate(
        [
            router_weight.astype(BF16),
            own_gains,
            jnp.zeros((shard_rows, LANES - EXPERTS - 2), BF16),
        ],
        axis=1,
    )
    qkv_own = query_key_value_weight.astype(BF16)
    qkv_width = qkv_own.shape[1]
    half_width = qkv_width // 2
    attention_own = jnp.concatenate([qkv_own, small_part, out_weight.astype(BF16)], axis=1)
    attention_edges = (0, half_width, qkv_width + LANES, attention_own.shape[1])

    segments = segment_ids[0]
    named = jnp.concatenate([route_ids[0].T, segments[None]])
    named_x = swap(named, "x")
    named_core = swap(jnp.stack([named, named_x]), "core")
    routes_all = jnp.stack([part[:TOPK] for part in (named, named_x, *named_core)])
    seg_prev = named_x[TOPK]
    (top_sent,) = hold((top,), named_x) if staged else (top,)
    top_x = swap(top_sent, "x")

    pair = expert_pairs(expert_in, expert_down)
    gather_z = lambda half: lax.all_gather(half, "z")
    if staged:
        attention_z = [rotate(attention_own, -k) for k in range(1, Z_STEPS)]
        own_one, sent_one = expert_halves(pair, 0, in_rows)
        first_held, second_held, out_held = (
            jnp.stack([part[:, start:end] for part in (attention_own, *attention_z)])
            for start, end in zip(attention_edges, attention_edges[1:])
        )
        first_held, second_held, own_one, seg_prev, routes_all = hold(
            (first_held, second_held, own_one, seg_prev, routes_all), sent_one
        )
        one_own = gather_z(own_one)
        first_x = swap(first_held, "x")
        second_y = swap(second_held, "y")
        other_one = swap(sent_one, "x")
        first_held = jnp.stack([first_held, first_x])
        second_held = jnp.stack([second_held, second_y])
        first_held, other_one, top_x = hold((first_held, other_one, top_x))
        first_y = swap(first_held, "y")
        second_x = swap(second_held, "x")
        one_other = gather_z(other_one)
        first_held = jnp.stack([first_held, first_y])
        second_held = jnp.stack([second_held, second_x], axis=1)
        qkv_held = jnp.concatenate([first_held, second_held], axis=-1)
        (out_held,) = hold((out_held,), first_y, second_x)
        own_two, sent_two = expert_halves(pair, 1, in_rows)
        qkv_held, one_own, own_two = hold((qkv_held, one_own, own_two))
        out_x = swap(out_held, "x")
        qkv_core = swap(qkv_held, "core")
        one_own_y = swap(one_own, "y")
        qkv_pair = (qkv_held, qkv_core)
    else:
        qkv_pair, out_pair = (
            gather_whole(part)
            for part in (
                attention_own[:, : qkv_width + LANES],
                attention_own[:, qkv_width + LANES :],
            )
        )
        pieces_one, pieces_two = (gather_expert_whole(pair, i, in_rows) for i in range(2))

    half_size = HEAD_DIMENSION // 2
    positions = (x_index * local_rows + jnp.arange(local_rows, dtype=jnp.int32)).astype(F32)
    frequency = ROPE_BASE ** (-2.0 * jnp.arange(half_size, dtype=F32) / HEAD_DIMENSION)
    angles = positions[:, None] * frequency[None, :]
    cosine, sine = jnp.cos(angles), jnp.sin(angles)
    cosine = jnp.concatenate([cosine, cosine], axis=1)
    sine_forward = jnp.concatenate([-sine, sine], axis=1)
    half = x_index.astype(jnp.int32).reshape(1)

    experts_here = first_expert + jnp.arange(OWN_EXPERTS, dtype=jnp.int32)
    member = jnp.any(routes_all[None] == experts_here[:, None, None, None], axis=2)
    earlier = (
        lax.broadcasted_iota(jnp.int32, (local_rows, local_rows), 0)
        < lax.broadcasted_iota(jnp.int32, (local_rows, local_rows), 1)
    ).astype(BF16)
    rank = jnp.dot(
        member.astype(BF16).reshape(-1, local_rows), earlier, preferred_element_type=F32
    ).reshape(member.shape)
    rank = jnp.where(member, rank.astype(jnp.int32), -1)

    queries, kv_own, normed, qkv_low, small_low = project(
        where, x_tokens, qkv_pair, cosine, sine_forward
    )
    kv_prev = swap(kv_own, "x")
    attn_gain = small_low[:, EXPERTS].astype(F32)
    ffn_gain = small_low[:, EXPERTS + 1].astype(F32)
    router_rows = small_low.T[:16]
    if staged:
        kv_prev, out_x, one_own_y, one_other, sent_two = hold(
            (kv_prev, out_x, one_own_y, one_other, sent_two)
        )
        out_held = jnp.stack([out_held, out_x])
        out_y = swap(out_held, "y")
        other_two = swap(sent_two, "x")
        two_own = gather_z(own_two)
    segs = (segments[:, None], segments[None, :], seg_prev[None, :])
    attended, log_sums = attend(queries, kv_own, kv_prev, *segs, half)
    top_core, top_both = swap(top, "core"), swap(top_x, "core")
    if staged:
        attended, out_y, two_own, other_two = hold((attended, out_y, two_own, other_two))
        out_held = jnp.stack([out_held, out_y])
        out_pair = (out_held, swap(out_held, "core"))
        one_other_y = swap(one_other, "y")
        two_other = gather_z(other_two)
    middle, normed_ffn, second_scale, out_low = join(
        where, attended, x_tokens, ffn_gain[None, :], out_pair
    )

    ffn_core = swap(normed_ffn, "core")
    ffn_x = swap(normed_ffn, "x")
    if staged:
        two_own_y = swap(two_own, "y")
    ffn_both = swap(ffn_x, "core")
    x_all = (normed_ffn, ffn_x, ffn_core, ffn_both)
    t_all = (top, top_x, top_core, top_both)
    places = [jnp.concatenate([where, first_expert[None] + i]) for i in range(OWN_EXPERTS)]
    if staged:
        two_other, ffn_both = hold((two_other, ffn_both))
        x_all = (normed_ffn, ffn_x, ffn_core, ffn_both)
        pieces_one = (one_own, one_other, one_own_y, one_other_y)
        pieces_two = (two_own, two_other, two_own_y, swap(two_other, "y"))

    def expert(i, pieces, sources, given, gives, grads_too):
        some = lambda parts: [parts[s] for s in sources]
        ranks = (
            jnp.stack(some(rank[i]))[:, None, :],
            jnp.stack(some(rank[i]))[:, :, None],
        )
        return expert_pass(
            places[i], pieces, some(x_all), some(t_all), ranks, router_rows, given, gives, grads_too
        )

    mix_one, ffn_one, gates_one, _, grads_one = expert(
        0, pieces_one, (0, 1, 2, 3), (), False, True
    )
    if staged:
        back_one = [swap(part, "y") for part in grads_one[2:]]
        pieces_two = hold(pieces_two, gates_one)
    mix_far, ffn_far, gates_far, kept_far, _ = expert(1, pieces_two, (1, 3), (), True, False)
    add = lambda *parts: sum(part.astype(F32) for part in parts)
    ffn_come = swap(add(ffn_one[3], ffn_far[1]).astype(BF16), "core")
    ffn_crossed = swap(add(ffn_one[1], ffn_far[0], ffn_come).astype(BF16), "x")
    if staged:
        total_one = [add(grads_one[0], back_one[0]).astype(BF16)]
        kept_far[0], total_one[0] = hold((kept_far[0], total_one[0]), ffn_come)
        sums_one = [lax.psum_scatter(total_one[0], "z", scatter_dimension=0)]
    mix_near, ffn_near, gates_near, _, grads_two = expert(
        1, pieces_two, (0, 2), tuple(kept_far), False, True
    )
    gates_two = jnp.stack([gates_near[0], gates_far[0], gates_near[1], gates_far[1]])

    if staged:
        back_two = [swap(part, "y") for part in grads_two[2:]]
        total_one.append(add(grads_one[1], back_one[1]).astype(BF16))
        sums_one.append(lax.psum_scatter(total_one[1], "z", scatter_dimension=0))
    else:
        sums_one, sums_two = (scatter_expert_whole(grads) for grads in (grads_one, grads_two))
    ffn_back, ffn_crossed = hold((ffn_near[1], ffn_crossed))
    ffn_arrived = swap(add(ffn_one[2], ffn_back).astype(BF16), "core")
    gate_grad = jnp.concatenate([gates_one, gates_two], axis=1)
    spread = lax.dynamic_update_slice_in_dim(
        jnp.zeros((SOURCES, EXPERTS, local_rows), F32), gate_grad, first_expert, axis=1
    )
    spread_core = swap(spread[2:], "core")
    spread_x = swap(spread[1] + spread_core[1], "x")
    prob_grad = (spread[0] + spread_core[0] + spread_x).T
    if staged:
        ffn_crossed, sums_one[0] = hold((ffn_crossed, sums_one[0]), total_one[1])
    ffn_grad = add(ffn_one[0], ffn_near[0], ffn_arrived, ffn_crossed)
    (mix_sent,) = hold((mix_far[1],), ffn_crossed)
    mix_come = swap(add(mix_one[3], mix_sent).astype(BF16), "core")
    mix_arrived = swap(add(mix_one[2], mix_near[1]).astype(BF16), "core")
    mix_crossed = swap(add(mix_one[1], mix_far[0], mix_come).astype(BF16), "x")

    logits = jnp.dot(normed_ffn, small_low[:, :EXPERTS], preferred_element_type=F32)
    exponent = jnp.exp(logits - jnp.max(logits, axis=-1, keepdims=True))
    router_probs = exponent / jnp.sum(exponent, axis=-1, keepdims=True)
    logit_grad = router_probs * (
        prob_grad - jnp.sum(router_probs * prob_grad, axis=-1, keepdims=True)
    )
    router_grad = jnp.dot(normed_ffn.astype(F32).T, logit_grad, precision=PRECISE)
    ffn_grad = ffn_grad + jnp.dot(
        logit_grad, small_low[:, :EXPERTS].astype(F32).T, precision=PRECISE
    )
    ffn_gain_grad = jnp.sum(middle * second_scale * ffn_grad, axis=0)
    middle_grad = top.astype(F32) + norm_value_grad(middle, second_scale, ffn_gain, ffn_grad)
    branch_grad = middle_grad.astype(BF16)
    attended_grad = dot_nt(branch_grad, out_low).astype(BF16)
    small_grad = jnp.concatenate(
        [
            router_grad,
            ffn_gain_grad[:, None],
            jnp.zeros((model_width, LANES - EXPERTS - 1), F32),
        ],
        axis=1,
    )
    (out_blocks,) = grad_rows(
        where.at[1].set(0),
        attended, (branch_grad,),
        small_grad,
        (0, model_width + LANES),
    )
    if staged:
        attended_grad, back_two[0] = hold((attended_grad, back_two[0]), out_blocks[1])
        total_two = [add(grads_two[0], back_two[0]).astype(BF16)]
        sums_two = [lax.psum_scatter(total_two[0], "z", scatter_dimension=0)]
        out_kept, out_sent = kept_sent(fold(*out_blocks, "core"), "y")
        out_come = swap(out_sent.astype(BF16), "y")
    query_grad, key_own, value_own, key_prev, value_prev = attend_back(
        queries, kv_own, kv_prev, *segs, half, attended_grad, log_sums, cosine, -sine_forward
    )
    crossed = swap(jnp.concatenate([key_prev, value_prev], axis=1).astype(BF16), "x")
    if staged:
        crossed, back_two[1] = hold((crossed, back_two[1]), query_grad)
        total_two.append(add(grads_two[1], back_two[1]).astype(BF16))
        sums_two.append(lax.psum_scatter(total_two[1], "z", scatter_dimension=0))
    crossed = crossed.astype(F32)
    key_grad = (key_own + crossed[:, :key_width]).astype(BF16).astype(F32)
    value_grad = value_own + crossed[:, key_width:]
    key_grad = key_grad.reshape(local_rows, KEY_VALUE_HEADS, HEAD_DIMENSION)
    key_grad = key_grad * cosine[:, None, :] - jnp.roll(key_grad, half_size, axis=2) * sine_forward[
        :, None, :
    ]
    kv_grad = jnp.concatenate(
        [key_grad.reshape(local_rows, key_width).astype(BF16), value_grad.astype(BF16)], axis=1
    )
    if staged:
        kv_grad, out_come, sums_one[1], mix_crossed = hold(
            (kv_grad, out_come, sums_one[1], mix_crossed)
        )
        out_kept, out_sent = kept_sent(out_kept + out_come.astype(F32), "x")
        out_come = swap(out_sent.astype(BF16), "x")
    qkv_blocks = grad_rows(
        where.at[1].set(0), normed, (query_grad, kv_grad), None, (0, half_width, 2 * half_width)
    )
    if staged:
        (out_come,) = hold((out_come,), qkv_blocks[0][1])
        first = fold(*qkv_blocks[0], "core")
        second = fold(*qkv_blocks[1], "core")
        first_kept, first_sent = kept_sent(first, "y")
        second_kept, second_sent = kept_sent(second, "x")
        first_come = swap(first_sent.astype(BF16), "y")
        second_come = swap(second_sent.astype(BF16), "x")
        first_kept, first_sent = kept_sent(first_kept + first_come.astype(F32), "x")
        second_kept, second_sent = kept_sent(second_kept + second_come.astype(F32), "y")
        (out_come,) = hold((out_come,), first_come, second_come, total_two[1])
        out_total = (out_kept + out_come.astype(F32)).astype(BF16)
        first_come = swap(first_sent.astype(BF16), "x")
        second_come = swap(second_sent.astype(BF16), "y")
        *sums_one, sums_two[0], sums_two[1] = hold(
            (*sums_one, *sums_two), first_come, second_come
        )
        expert_sums = [finish_expert(sums, in_rows) for sums in (sums_one, sums_two)]
        first = first_kept + first_come.astype(F32)
        second = second_kept + second_come.astype(F32)
        rows_total = jnp.concatenate([first.astype(BF16), second.astype(BF16), out_total], axis=-1)
        rows_sum = lax.psum_scatter(rows_total, "z", scatter_dimension=0).astype(F32)
        qkv_sum, out_rows = rows_sum[:, :qkv_width], rows_sum[:, qkv_width:]
    else:
        expert_sums = [finish_expert(sums, in_rows) for sums in (sums_one, sums_two)]
        out_rows = scatter_whole(*out_blocks)
        qkv_sum = jnp.concatenate([scatter_whole(*blocks) for blocks in qkv_blocks], axis=1)
    in_sum, down_sum = (jnp.stack(parts, axis=2) for parts in zip(*expert_sums))
    in_sum = in_sum.reshape(expert_in.shape)
    down_sum = down_sum.reshape(expert_down.shape)
    mixture = add(mix_one[0], mix_near[0], mix_arrived, mix_crossed)
    output = (middle + mixture).astype(BF16)
    mixed_grad = jnp.concatenate([query_grad, kv_grad], axis=1)
    inputs = x_tokens.astype(F32)
    input_grad = middle_grad + norm_value_grad(
        inputs, rms_scale(inputs), attn_gain, dot_nt(mixed_grad, qkv_low)
    )

    out_sum = out_rows[:, :model_width]
    router_sum = out_rows[:, model_width : model_width + EXPERTS]
    attn_gain_sum = jnp.sum(qkv_sum * qkv_own.astype(F32), axis=1) / own_gains[:, 0].astype(F32)
    gains_sum = jnp.stack([attn_gain_sum, out_rows[:, model_width + EXPERTS]], axis=1)

    square_total = (
        jnp.sum(qkv_sum * qkv_sum)
        + jnp.sum(out_sum * out_sum)
        + jnp.sum(router_sum * router_sum)
        + jnp.sum(in_sum * in_sum)
        + jnp.sum(down_sum * down_sum)
        + jnp.sum(gains_sum * gains_sum)
    )
    grad_norm = jnp.sqrt(total_over(square_total))
    factor = CLIP_NORM / jnp.maximum(grad_norm, CLIP_NORM)
    new_weights, new_moments, new_seconds = update_all(
        (query_key_value_weight, out_weight, router_weight, expert_in, expert_down, norm_gains),
        (qkv_sum, out_sum, router_sum, in_sum, down_sum, gains_sum),
        (query_key_value_moment, out_moment, router_moment, in_moment, down_moment, gains_moment),
        (query_key_value_second, out_second, router_second, in_second, down_second, gains_second),
        factor,
    )
    return (
        output[None],
        input_grad.astype(BF16)[None],
        grad_norm,
        *new_weights,
        *new_moments,
        *new_seconds,
    )


def solution(mesh):
    mesh = jax.sharding.Mesh(
        mesh.devices.reshape(mesh.shape["seq"], mesh.shape["fsdp"] // 4, 2, 2), ALL_AXES
    )
    token_spec = P(ROWS, "x", None)
    row_spec = P(ALL_AXES, None)
    expert_spec = P(None, ALL_AXES, None)
    state_specs = (row_spec, row_spec, row_spec, expert_spec, expert_spec, row_spec)
    return jax.shard_map(
        shards,
        mesh=mesh,
        in_specs=(token_spec, token_spec, P(ROWS, "x"), token_spec) + state_specs * 3,
        out_specs=(token_spec, token_spec, P()) + state_specs * 3,
        check_vma=False,
    )
```
